256 devices in a mesh: seq: 4 (over z_lo), row: 8 (over x, core), col: 8 (over y, z_hi).
Axes of the slice: x: 4, y: 4, z: 8 (z_hi: 2, z_lo: 4; z = z_hi * 4 + z_lo), core: 2. Of those that a mesh axis runs over, the one named last changes fastest.
Arguments:
- layernormed_alignment: bfloat16 [128, 1536, 64], P('seq', 'row'), may hold values from -6 to 6
- average_cotangent: bfloat16 [128, 1536, 64], P('seq', 'row'), may hold values from -6 to 6
- sequence_validity: int32 [128, 1536], P('seq', 'row'), may hold values 0 or 1
- residue_validity: int32 [1536], replicated, may hold values 0 or 1
- pair_scores: float32 [8, 1536, 1536], P(None, 'row', 'col'), may hold values from -12 to 280
- payload_projection: bfloat16 [64, 256], replicated, may hold values from -0.75 to 0.75
- sigmoid_projection: bfloat16 [64, 256], replicated, may hold values from -0.75 to 0.75
- final_projection: bfloat16 [256, 64], replicated, may hold values from -0.375 to 0.375
Outputs:
- alignment_cotangent: float32 [128, 1536, 64], P('seq', ('row', 'col'))
- score_cotangent: float32 [8, 1536, 1536], P('seq', 'row', 'col')
The draws below stay inside these ranges and needn't reach their ends.
All inputs are finite; a program needn't handle non-finite values. No bound on the sum of `sequence_validity` on one device may be relied on, other than what follows from the above.
Results may differ from the reference program's by a relative error of at most 0.0041.
Values may be sent and summed in bfloat16 or wider, within the bound.
No kernel may reach another device: no remote copies, remote signals or barrier semaphores. Data moves between devices by JAX's collectives and lax.ppermute only.
A program may use at most 128 MiB of HBM per device.

```python
import jax
import jax.numpy as jnp
from jax import lax

ALIGN_FEATURES = 64
ATTENDER_COUNT = 8
FEATURES_ON_ONE = 32
RESIDUE_COUNT = 1536
SEQUENCE_NUMBER = 128


def draw_pair_scores(key, part):
    key = jax.random.fold_in(key, 11)
    key_base = jax.random.fold_in(key, 0)
    base = jnp.clip(jax.random.normal(key_base, (ATTENDER_COUNT, RESIDUE_COUNT, RESIDUE_COUNT), jnp.float32) * 2.0, -12.0, 12.0)
    return base


def place_ends(result, stream_key, smallest, largest):
    shape = result.shape
    index_at = [jax.random.randint(jax.random.fold_in(stream_key, axis), (), 0, shape[axis]) for axis in range(len(shape))]
    result = result.at[tuple(index_at)].set(smallest)
    longest = shape.index(max(shape))
    index_at[longest] = (index_at[longest] + 1) % shape[longest]
    return result.at[tuple(index_at)].set(largest)


def block_levels(own_key, shape, cuts, low, high):
    def one(position, shards_of):
        steps = jax.random.uniform(jax.random.fold_in(jax.random.fold_in(own_key, 6), position), (shards_of,), jnp.float32, low / len(cuts), high / len(cuts))
        return jnp.repeat(jnp.exp(steps), shape[position] // shards_of).reshape((-1,) + (1,) * (len(shape) - position - 1))

    level = one(*cuts[0])
    for cut in cuts[1:]:
        level = level * one(*cut)
    return level


def centred(rng, shape, deviation, most, shards=(), kind=jnp.bfloat16):
    loudness = block_levels(rng, shape, shards, -0.22, 0.18) if shards else 1.0
    drawn = jax.random.normal(rng, shape, jnp.float32) * deviation * loudness
    return jnp.minimum(jnp.maximum(drawn, -most), most).astype(kind)


def setup_inputs(seed: int = 0) -> dict:
    key_list = jax.random.split(jax.random.key(seed), 9)
    layernormed_alignment = centred(key_list[0], (SEQUENCE_NUMBER, RESIDUE_COUNT, ALIGN_FEATURES), 1.0, 6.0, ((0, 4), (1, 8)))
    average_cotangent = centred(key_list[1], (SEQUENCE_NUMBER, RESIDUE_COUNT, ALIGN_FEATURES), 1.0, 6.0, ((0, 4), (1, 8)))
    sequence_validity = place_ends((jax.random.randint(key_list[2], (SEQUENCE_NUMBER, RESIDUE_COUNT), 0, 4) < 3).astype(jnp.int32), jax.random.fold_in(key_list[2], 1), 0, 1)
    residue_validity = place_ends((jax.random.randint(key_list[3], (RESIDUE_COUNT,), 0, 8) < 7).astype(jnp.int32), jax.random.fold_in(key_list[3], 1), 0, 1)
    pair_scores = draw_pair_scores(jax.random.fold_in(key_list[8], 71), 0)
    payload_projection = centred(key_list[5], (ALIGN_FEATURES, ATTENDER_COUNT * FEATURES_ON_ONE), ALIGN_FEATURES ** -0.5, 0.75)
    sigmoid_projection = centred(key_list[6], (ALIGN_FEATURES, ATTENDER_COUNT * FEATURES_ON_ONE), ALIGN_FEATURES ** -0.5, 0.75)
    final_projection = centred(key_list[7], (ATTENDER_COUNT * FEATURES_ON_ONE, ALIGN_FEATURES), (ATTENDER_COUNT * FEATURES_ON_ONE) ** -0.5, 0.375)
    return {"layernormed_alignment": layernormed_alignment, "average_cotangent": average_cotangent, "sequence_validity": sequence_validity, "residue_validity": residue_validity, "pair_scores": pair_scores, "payload_projection": payload_projection, "sigmoid_projection": sigmoid_projection, "final_projection": final_projection}


def reference(layernormed_alignment, average_cotangent, sequence_validity, residue_validity, pair_scores, payload_projection, sigmoid_projection, final_projection):
    collected_sequences = SEQUENCE_NUMBER * RESIDUE_COUNT
    merged_layout = layernormed_alignment.reshape(collected_sequences, ALIGN_FEATURES)
    values = jnp.dot(merged_layout, payload_projection, preferred_element_type=jnp.float32).astype(jnp.bfloat16)
    values = lax.optimization_barrier(values)
    gate_act = jax.nn.sigmoid(jnp.dot(merged_layout, sigmoid_projection, preferred_element_type=jnp.float32))
    projection_cotangent = jnp.dot(average_cotangent.reshape(collected_sequences, ALIGN_FEATURES), final_projection.T, preferred_element_type=jnp.float32)
    kept_sequences = sequence_validity.reshape(collected_sequences, 1).astype(jnp.float32)
    d_att = lax.optimization_barrier((projection_cotangent * gate_act * kept_sequences).astype(jnp.bfloat16))
    gate_term = projection_cotangent * kept_sequences * gate_act * (1.0 - gate_act)
    keep_cols = residue_validity > 0

    def by_head(incoming_array):
        return incoming_array.reshape(SEQUENCE_NUMBER, RESIDUE_COUNT, ATTENDER_COUNT, FEATURES_ON_ONE).transpose(2, 0, 1, 3)

    def one_head(pieces):
        bias, values_h, d_att_h, gate_h = pieces
        masked = jnp.where(keep_cols[None, :], bias, jnp.float32(-1e9))
        peak = jnp.max(masked, axis=1, keepdims=True)
        expon = jnp.exp(masked - peak)
        weights = expon / jnp.sum(expon, axis=1, keepdims=True)
        w_round = lax.optimization_barrier(weights.astype(jnp.bfloat16)).astype(jnp.float32)
        val_wide = values_h.astype(jnp.float32)
        att_wide = d_att_h.astype(jnp.float32)
        average = jnp.einsum('ij,sjc->sic', w_round, val_wide)
        payload_cotangent = jnp.einsum('ij,sic->sjc', w_round, att_wide)
        d_weights = jnp.einsum('sic,sjc->ij', att_wide, val_wide)
        inner = jnp.sum(weights * d_weights, axis=1, keepdims=True)
        return weights * (d_weights - inner), payload_cotangent, gate_h * average

    score_cotangent, payload_cotangent, sigmoid_cotangent = lax.map(one_head, (pair_scores, by_head(values), by_head(d_att), by_head(gate_term)))

    def merge_front_axes(incoming_array):
        return incoming_array.transpose(1, 2, 0, 3).reshape(collected_sequences, ATTENDER_COUNT * FEATURES_ON_ONE)

    alignment_cotangent = jnp.dot(merge_front_axes(payload_cotangent), payload_projection.astype(jnp.float32).T, precision=lax.Precision.HIGHEST)
    alignment_cotangent = alignment_cotangent + jnp.dot(merge_front_axes(sigmoid_cotangent), sigmoid_projection.astype(jnp.float32).T, precision=lax.Precision.HIGHEST)
    return alignment_cotangent.reshape(SEQUENCE_NUMBER, RESIDUE_COUNT, ALIGN_FEATURES), score_cotangent
```

```python
import jax
import jax.numpy as jnp
from jax import lax
from jax.experimental import pallas as pl
from jax.experimental.pallas import tpu as pltpu
from jax.sharding import PartitionSpec as P

F32 = jnp.float32
BF16 = jnp.bfloat16
MASKED = -1000000000.0
VMEM_BYTES = 24 * 1024 * 1024
STEPS = 4


def call(kernel, outs, inputs, in_specs=None, out_specs=None, grid=None, scratch=(), scalars=None, flops=0, moved=0):
    local = lambda: pl.BlockSpec(memory_space=pltpu.VMEM)
    several = isinstance(outs, list)
    operands = [] if scalars is None else [scalars]
    if in_specs is None:
        in_specs = [local() for _ in inputs]
    if out_specs is None:
        out_specs = [local() for _ in outs] if several else local()
    extra = {} if grid is None else {"grid": grid}
    return pl.pallas_call(
        kernel,
        out_shape=outs,
        in_specs=[pl.BlockSpec(memory_space=pltpu.SMEM)] * len(operands) + in_specs,
        out_specs=out_specs,
        scratch_shapes=list(scratch),
        compiler_params=pltpu.CompilerParams(vmem_limit_bytes=VMEM_BYTES),
        cost_estimate=pl.CostEstimate(flops=flops, bytes_accessed=moved, transcendentals=0),
        **extra,
    )(*operands, *inputs)


def whole(shape):
    return pl.BlockSpec(shape, lambda i: (0,) * len(shape))


def by_step(*dims):
    return pl.BlockSpec(dims, lambda i: (i,) + (0,) * (len(dims) - 1))


def far(a):
    return pltpu.with_memory_space_constraint(a, pltpu.HBM)


def dot(a, b):
    return jnp.dot(a, b, preferred_element_type=F32)


def turned(a):
    return a.astype(F32).T.astype(a.dtype)


def open_kernel(x_ref, scores_ref, keep_ref, out_ref, stats_ref):
    sequences = x_ref.shape[0]
    half = sequences // 2
    out_ref[0:sequences] = x_ref[:, :, 0:128]
    out_ref[sequences:] = jnp.concatenate([x_ref[0:half, :, 128:192], x_ref[half:, :, 128:192]], axis=-1)
    heads, rows, _ = scores_ref.shape
    keep = keep_ref[...] > 0
    lane = lax.broadcasted_iota(jnp.int32, (rows, 128), 1)
    table = jnp.zeros((rows, 128), F32)
    for h in range(heads):
        masked = jnp.where(keep, scores_ref[h], MASKED)
        peak = jnp.max(masked, axis=1, keepdims=True)
        total = jnp.sum(jnp.exp(masked - peak), axis=1, keepdims=True)
        table = jnp.where(lane == h, peak, table)
        table = jnp.where(lane == heads + h, total, table)
    packed = table.T[0 : 2 * heads]
    for k in range(stats_ref.shape[0]):
        stats_ref[k] = packed


def gate_kernel(x_ref, cot_ref, mask_ref, gate_w_ref, final_w_ref, att_ref, term_ref, att_rows_ref, wt):
    @pl.when(pl.program_id(0) == 0)
    def _():
        wt[0] = turned(gate_w_ref[...])
        wt[1] = turned(final_w_ref[...])

    sequences, _, rows = x_ref.shape
    heads = att_rows_ref.shape[0]
    dim = wt.shape[1] // heads
    mask = mask_ref[...].astype(F32)
    for s in range(sequences):
        gate = 1.0 / (1.0 + jnp.exp(-dot(wt[0], x_ref[s])))
        cot = dot(wt[1], cot_ref[s]) * mask[s : s + 1]
        att = cot * gate
        att_ref[s] = att.astype(BF16)
        term_ref[s] = att * (1.0 - gate)
    for h in range(heads):
        block = att_ref[:, h * dim : (h + 1) * dim, :].reshape(sequences * dim, rows)
        att_rows_ref[h] = turned(block)


def project_rows(weight, hi, lo, out_ref, first=None):
    sequences = hi.shape[0]
    chunks, stretch, _ = out_ref.shape
    features = weight.shape[0]
    for s in range(0, sequences, 2):
        pair = [dot(weight, hi[s + k]) + dot(weight, lo[s + k]) for k in (0, 1)]
        wide = jnp.concatenate(pair, axis=0).T.reshape(chunks, stretch, 2 * features).astype(out_ref.dtype)
        if first is None:
            out_ref[:, :, s * features : (s + 2) * features] = wide
        else:
            out_ref[:, :, pl.ds(pl.multiple_of((first + s) * features, 128), 2 * features)] = wide


def split(grad, hi, lo, h, dim):
    top = grad.astype(BF16)
    hi[:, h * dim : (h + 1) * dim, :] = top
    lo[:, h * dim : (h + 1) * dim, :] = (grad - top.astype(F32)).astype(BF16)


def column_kernel(
    scores_ref, keep_ref, stats_ref, att_ref, payload_ref, weights_ref, turned_ref, out_ref, wb, hi, lo
):
    heads, rows, columns = scores_ref.shape
    sequences, width, _ = att_ref.shape
    dim = width // heads

    @pl.when(pl.program_id(0) == 0)
    def _():
        peaks = stats_ref[:, 0:heads]
        peak = jnp.max(peaks, axis=0)
        total = jnp.sum(stats_ref[:, heads : 2 * heads] * jnp.exp(peaks - peak[None]), axis=0)
        table = jnp.concatenate([peak, 1.0 / total, jnp.zeros((128 - 2 * heads, rows), F32)], axis=0).T
        keep = keep_ref[...] > 0
        for h in range(heads):
            masked = jnp.where(keep, scores_ref[h], MASKED)
            weights = jnp.exp(masked - table[:, h : h + 1]) * table[:, heads + h : heads + h + 1]
            weights_ref[h] = weights
            wb[h] = weights.astype(BF16)
            turned_ref[h] = weights.T.astype(BF16)

    for h in range(heads):
        block = att_ref[:, h * dim : (h + 1) * dim, :].reshape(sequences * dim, rows)
        split(dot(block, wb[h]).reshape(sequences, dim, columns), hi, lo, h, dim)
    project_rows(payload_ref[...], hi, lo, out_ref)


def row_kernel(
    place_ref,
    mine_ref,
    other_ref,
    payload_ref,
    gate_w_ref,
    turned_ref,
    weights_ref,
    term_ref,
    att_rows_ref,
    inner_ref,
    row0_ref,
    row1_ref,
    row2_ref,
    row3_ref,
    pair0_ref,
    pair1_ref,
    pair2_ref,
    pair3_ref,
    wt,
    values,
    hi,
    lo,
    row_out,
    pair_sum,
    pair_out,
):
    step = pl.program_id(0)
    group, width, rows = term_ref.shape
    heads, columns, _ = turned_ref.shape
    dim = width // heads
    sequences = mine_ref.shape[0] * 2 // 3
    half = sequences // 2

    @pl.when(step == 0)
    def _():
        wt[...] = turned(payload_ref[...])
        pair_sum[...] = jnp.zeros(pair_sum.shape, F32)

    first = pl.multiple_of(step * group, group)
    late = first >= half
    shared = sequences + first - jnp.where(late, half, 0)
    own = place_ref[0] == place_ref[1]
    main = jnp.where(own, mine_ref[pl.ds(first, group)], other_ref[pl.ds(first, group)])
    tail = jnp.where(own, mine_ref[pl.ds(shared, group)], other_ref[pl.ds(shared, group)])
    tail = jnp.where(late, tail[:, :, 64:128], tail[:, :, 0:64])
    for k in range(group):
        tokens = jnp.concatenate([main[k], tail[k]], axis=-1)
        values[k] = dot(wt[...], tokens).astype(BF16)
    for h in range(heads):
        block = values[:, h * dim : (h + 1) * dim, :].reshape(group * dim, columns)
        average = dot(block, turned_ref[h]).reshape(group, dim, rows)
        split(average * term_ref[:, h * dim : (h + 1) * dim, :], hi, lo, h, dim)
        pair_sum[h] += dot(att_rows_ref[h], block)
    project_rows(gate_w_ref[...], hi, lo, row_out, first)

    @pl.when(step == pl.num_programs(0) - 1)
    def _():
        for k, out_ref in enumerate((row0_ref, row1_ref, row2_ref, row3_ref)):
            out_ref[...] = row_out[pl.ds(2 * (place_ref[2] ^ k), 2)]
        lane = lax.broadcasted_iota(jnp.int32, (rows, 128), 1)
        table = jnp.zeros((rows, 128), F32)
        owners = pair_out.shape[0]
        own_heads = heads // owners
        for k in range(owners):
            tails = []
            for g in range(own_heads):
                h = k * own_heads + g
                grad = pair_sum[h].astype(BF16)
                pair_out[k, g] = grad[:, 0:128]
                tails.append(grad[:, 128:192])
                inner = jnp.sum(weights_ref[h] * grad.astype(F32), axis=1, keepdims=True)
                table = jnp.where(lane == h, inner, table)
            pair_out[k, own_heads] = jnp.concatenate(tails, axis=-1)
        inner_ref[...] = table.T[0:heads]
        for k, out_ref in enumerate((pair0_ref, pair1_ref, pair2_ref, pair3_ref)):
            out_ref[...] = pair_out[place_ref[3] ^ k]


def score_kernel(
    place_ref,
    part0_ref,
    part1_ref,
    part2_ref,
    part3_ref,
    inner0_ref,
    inner1_ref,
    inner2_ref,
    inner3_ref,
    weights_ref,
    out_ref,
):
    heads, rows, _ = out_ref.shape
    total = part0_ref[...].astype(F32)
    for part in (part1_ref, part2_ref, part3_ref):
        total = total + part[...].astype(F32)
    inner = (inner0_ref[...] + inner1_ref[...]) + (inner2_ref[...] + inner3_ref[...])
    table = jnp.concatenate([inner, jnp.zeros((128 - inner.shape[0], rows), F32)], axis=0).T
    lane = lax.broadcasted_iota(jnp.int32, table.shape, 1)
    for h in range(heads):
        mine = place_ref[3] * heads + h
        grad = jnp.concatenate([total[h], total[heads][:, 64 * h : 64 * h + 64]], axis=-1)
        own = jnp.sum(jnp.where(lane == mine, table, 0.0), axis=1, keepdims=True)
        out_ref[h] = weights_ref[mine] * (grad - own)


def fold_kernel(place_ref, part0_ref, part1_ref, part2_ref, part3_ref, cols_ref, keep_ref, send_ref):
    total = part0_ref[...].astype(F32)
    for part in (part1_ref, part2_ref, part3_ref):
        total = total + part[...].astype(F32)
    high = place_ref[1] == 1
    keep_ref[...] = jnp.where(high, total[1], total[0]) + cols_ref[...].astype(F32)
    send_ref[...] = jnp.where(high, total[0], total[1]).astype(BF16)


def join_kernel(keep_ref, rows_ref, out_ref):
    sequences, _, features = out_ref.shape
    total = keep_ref[...] + rows_ref[...].astype(F32)
    for s in range(sequences):
        out_ref[s] = total[:, s * features : (s + 1) * features]


def body(
    layernormed_alignment,
    average_cotangent,
    sequence_validity,
    residue_validity,
    pair_scores,
    payload_projection,
    sigmoid_projection,
    final_projection,
):
    row_count = lax.axis_size("row")
    col_count = lax.axis_size("col")
    seq_count = lax.axis_size("seq")
    row_pos = lax.axis_index("row")
    col_pos = lax.axis_index("col")
    seq_pos = lax.axis_index("seq")
    sequences, rows, features = layernormed_alignment.shape
    heads, _, columns = pair_scores.shape
    width = payload_projection.shape[1]
    dim = width // heads
    stretch = rows // col_count
    wide = sequences * features
    own = heads // seq_count
    group = sequences // STEPS
    side = row_count // 2
    core, plane, across = row_pos % 2, col_pos % 2, col_pos // 2
    place = jnp.stack([core, plane, across, seq_pos]).astype(jnp.int32)

    tokens = far(jnp.swapaxes(layernormed_alignment, 1, 2))
    cotangent = far(jnp.swapaxes(average_cotangent, 1, 2))
    scores = far(pair_scores)
    payload_w = far(payload_projection)
    gate_w = far(sigmoid_projection)
    final_w = far(final_projection.T)
    keep = lax.dynamic_slice_in_dim(residue_validity, col_pos * columns, columns, 0).reshape(1, columns)

    packed, stats = call(
        open_kernel,
        [
            jax.ShapeDtypeStruct((sequences * 3 // 2, features, 128), BF16),
            jax.ShapeDtypeStruct((col_count, 2 * heads, rows), F32),
        ],
        [tokens, scores, keep],
        moved=4 << 20,
    )
    stats = lax.all_to_all(stats, "col", 0, 0, tiled=True)

    at = lambda x, core, y, z: (x * 2 + core) * col_count + y * 2 + z
    routes = [
        (at(a, z, b, z), at((b + 2 * a) % side, z, a, z))
        for a in range(side)
        for b in range(side)
        for z in range(2)
    ]
    mine = lax.ppermute(packed, ("row", "col"), routes)

    d_att, gate_term, att_rows = call(
        gate_kernel,
        [
            pltpu.HBM((sequences, width, rows), BF16),
            pltpu.HBM((sequences, width, rows), F32),
            pltpu.HBM((heads, rows, sequences * dim), BF16),
        ],
        [tokens, cotangent, far(sequence_validity), gate_w, final_w],
        [
            by_step(group, features, rows),
            by_step(group, features, rows),
            by_step(group, rows),
            whole((features, width)),
            whole((features, width)),
        ],
        [
            by_step(group, width, rows),
            by_step(group, width, rows),
            pl.BlockSpec((heads, rows, group * dim), lambda i: (0, 0, i)),
        ],
        grid=(STEPS,),
        scratch=[pltpu.VMEM((2, width, features), BF16)],
        flops=1 << 30,
        moved=14 << 20,
    )
    mine, stats, d_att = lax.optimization_barrier((mine, stats, d_att))
    other = lax.ppermute(mine, "row", [(i, i ^ 1) for i in range(row_count)])

    pieces = [pltpu.VMEM((group, width, rows), BF16)] * 2
    weights, weights_turned, col_term = call(
        column_kernel,
        [
            pltpu.HBM((heads, rows, columns), F32),
            pltpu.HBM((heads, columns, rows), BF16),
            jax.ShapeDtypeStruct((row_count, stretch, wide), BF16),
        ],
        [scores, keep, stats, far(d_att), payload_w],
        [
            whole(pair_scores.shape),
            whole((1, columns)),
            whole((col_count, 2 * heads, rows)),
            by_step(group, width, rows),
            whole((features, width)),
        ],
        [
            whole((heads, rows, columns)),
            whole((heads, columns, rows)),
            pl.BlockSpec((row_count, stretch, group * features), lambda i: (0, 0, i)),
        ],
        grid=(STEPS,),
        scratch=[pltpu.VMEM((heads, rows, columns), BF16)] + pieces,
        flops=1 << 30,
        moved=14 << 20,
    )
    weights, weights_turned = far(weights), far(weights_turned)
    col_term = lax.all_to_all(col_term, "row", 0, 0, tiled=True)
    col_term = jnp.sum(col_term.astype(F32), axis=0).astype(BF16)
    col_term = lax.ppermute(
        col_term,
        ("row", "col"),
        [(r * col_count + c, c * col_count + r) for r in range(row_count) for c in range(col_count)],
    )

    packed_shape = (sequences * 3 // 2, features, 128)
    inner, *sent = call(
        row_kernel,
        [jax.ShapeDtypeStruct((heads, rows), F32)]
        + [jax.ShapeDtypeStruct((2, stretch, wide), BF16)] * side
        + [jax.ShapeDtypeStruct((own + 1, rows, 128), BF16)] * seq_count,
        [mine, other, payload_w, gate_w, weights_turned, weights, far(gate_term), far(att_rows)],
        [
            whole(packed_shape),
            whole(packed_shape),
            whole((features, width)),
            whole((features, width)),
            whole((heads, columns, rows)),
            whole((heads, rows, columns)),
            by_step(group, width, rows),
            pl.BlockSpec((heads, rows, group * dim), lambda i: (0, 0, i)),
        ],
        [whole((heads, rows))]
        + [whole((2, stretch, wide)) for _ in range(side)]
        + [whole((own + 1, rows, 128)) for _ in range(seq_count)],
        grid=(STEPS,),
        scratch=[pltpu.VMEM((width, features), BF16), pltpu.VMEM((group, width, columns), BF16)]
        + pieces
        + [
            pltpu.VMEM((col_count, stretch, wide), BF16),
            pltpu.VMEM((heads, rows, columns), F32),
            pltpu.VMEM((seq_count, own + 1, rows, 128), BF16),
        ],
        scalars=place,
        flops=1 << 30,
        moved=18 << 20,
    )
    row_term, d_weights = sent[:side], sent[side:]

    def swapped(a, axis, bits):
        return lax.ppermute(a, axis, [(i, i ^ bits) for i in range(lax.axis_size(axis))])

    inner = inner + sum(swapped(inner, "col", 2 * k) for k in range(1, side))
    row_term = row_term[:1] + [swapped(row_term[k], "col", 2 * k) for k in range(1, side)]
    d_weights = d_weights[:1] + [swapped(d_weights[k], "seq", k) for k in range(1, seq_count)]
    row_keep, row_send = call(
        fold_kernel,
        [jax.ShapeDtypeStruct((stretch, wide), F32), jax.ShapeDtypeStruct((stretch, wide), BF16)],
        row_term + [col_term],
        scalars=place,
        moved=2 << 20,
    )
    inner = inner + swapped(inner, "col", 1)
    row_send = swapped(row_send, "col", 1)
    inner, *d_weights = lax.optimization_barrier((inner, *d_weights))
    inners = [inner] + [swapped(inner, "seq", k) for k in range(1, seq_count)]
    score_cotangent = call(
        score_kernel,
        jax.ShapeDtypeStruct((own, rows, columns), F32),
        d_weights + inners + [weights],
        scalars=place,
        moved=2 << 20,
    )

    alignment_cotangent = call(
        join_kernel,
        jax.ShapeDtypeStruct((sequences, stretch, features), F32),
        [row_keep, row_send],
        moved=2 << 20,
    )
    return (alignment_cotangent, score_cotangent)


def solution(mesh):
    return jax.shard_map(
        body,
        mesh=mesh,
        in_specs=(
            P("seq", "row", None),
            P("seq", "row", None),
            P("seq", "row"),
            P(),
            P(None, "row", "col"),
            P(),
            P(),
            P(),
        ),
        out_specs=(P("seq", ("row", "col"), None), P("seq", "row", "col")),
        check_vma=False,
    )
```

```python
import jax
import jax.numpy as jnp
from jax import lax
from jax.experimental import pallas as pl
from jax.experimental.pallas import tpu as pltpu
from jax.sharding import PartitionSpec as P

F32 = jnp.float32
BF16 = jnp.bfloat16
MASKED = -1000000000.0
VMEM_BYTES = 24 * 1024 * 1024
STEPS = 4


def call(kernel, outs, inputs, in_specs=None, out_specs=None, grid=None, scratch=(), scalars=None, flops=0, moved=0):
    local = lambda: pl.BlockSpec(memory_space=pltpu.VMEM)
    several = isinstance(outs, list)
    operands = [] if scalars is None else [scalars]
    if in_specs is None:
        in_specs = [local() for _ in inputs]
    if out_specs is None:
        out_specs = [local() for _ in outs] if several else local()
    extra = {} if grid is None else {"grid": grid}
    return pl.pallas_call(
        kernel,
        out_shape=outs,
        in_specs=[pl.BlockSpec(memory_space=pltpu.SMEM)] * len(operands) + in_specs,
        out_specs=out_specs,
        scratch_shapes=list(scratch),
        compiler_params=pltpu.CompilerParams(vmem_limit_bytes=VMEM_BYTES),
        cost_estimate=pl.CostEstimate(flops=flops, bytes_accessed=moved, transcendentals=0),
        **extra,
    )(*operands, *inputs)


def whole(shape):
    return pl.BlockSpec(shape, lambda i: (0,) * len(shape))


def by_step(*dims):
    return pl.BlockSpec(dims, lambda i: (i,) + (0,) * (len(dims) - 1))


def far(a):
    return pltpu.with_memory_space_constraint(a, pltpu.HBM)


def dot(a, b):
    return jnp.dot(a, b, preferred_element_type=F32)


def turned(a):
    return a.astype(F32).T.astype(a.dtype)


def stats_kernel(scores_ref, keep_ref, stats_ref):
    heads, rows, _ = scores_ref.shape
    keep = keep_ref[...] > 0
    lane = lax.broadcasted_iota(jnp.int32, (rows, 128), 1)
    table = jnp.zeros((rows, 128), F32)
    for h in range(heads):
        masked = jnp.where(keep, scores_ref[h], MASKED)
        peak = jnp.max(masked, axis=1, keepdims=True)
        total = jnp.sum(jnp.exp(masked - peak), axis=1, keepdims=True)
        table = jnp.where(lane == h, peak, table)
        table = jnp.where(lane == heads + h, total, table)
    packed = table.T[0 : 2 * heads]
    for k in range(stats_ref.shape[0]):
        stats_ref[k] = packed


def gate_kernel(x_ref, cot_ref, mask_ref, gate_w_ref, final_w_ref, att_ref, term_ref, att_rows_ref, wt):
    @pl.when(pl.program_id(0) == 0)
    def _():
        wt[0] = turned(gate_w_ref[...])
        wt[1] = turned(final_w_ref[...])

    sequences, _, rows = x_ref.shape
    heads = att_rows_ref.shape[0]
    dim = wt.shape[1] // heads
    mask = mask_ref[...].astype(F32)
    for s in range(sequences):
        gate = 1.0 / (1.0 + jnp.exp(-dot(wt[0], x_ref[s])))
        cot = dot(wt[1], cot_ref[s]) * mask[s : s + 1]
        att = cot * gate
        att_ref[s] = att.astype(BF16)
        term_ref[s] = (att * (1.0 - gate)).astype(BF16)
    for h in range(heads):
        block = att_ref[:, h * dim : (h + 1) * dim, :].reshape(sequences * dim, rows)
        att_rows_ref[h] = turned(block)


def project_rows(weight, hi, lo, out_ref, first):
    sequences = hi.shape[0]
    chunks, stretch, _ = out_ref.shape
    features = weight.shape[0]
    for s in range(0, sequences, 2):
        pair = [dot(weight, hi[s + k]) + dot(weight, lo[s + k]) for k in (0, 1)]
        rows = jnp.concatenate(pair, axis=0).T.reshape(chunks, stretch, 2 * features)
        lanes = pl.ds(pl.multiple_of((first + s) * features, 128), 2 * features)
        out_ref[:, :, lanes] = rows.astype(out_ref.dtype)


def split(grad, hi, lo, h, dim):
    top = grad.astype(BF16)
    hi[:, h * dim : (h + 1) * dim, :] = top
    lo[:, h * dim : (h + 1) * dim, :] = (grad - top.astype(F32)).astype(BF16)


def thirds(table):
    first = table.astype(BF16)
    rest = table - first.astype(F32)
    second = rest.astype(BF16)
    third = (rest - second.astype(F32)).astype(BF16)
    return jnp.concatenate([t.astype(F32) for t in (first, second, third)], axis=0).astype(BF16)


def joined(table):
    count = table.shape[0] // 3
    table = table.astype(F32)
    return table[0:count] + table[count : 2 * count] + table[2 * count : 3 * count]


def main_kernel(
    place_ref,
    scores_ref,
    keep_ref,
    stats_ref,
    att_ref,
    term_ref,
    att_rows_ref,
    mine_ref,
    other_ref,
    payload_ref,
    gate_w_ref,
    weights_ref,
    col_ref,
    row0_ref,
    row1_ref,
    row2_ref,
    row3_ref,
    pair0_ref,
    pair1_ref,
    pair2_ref,
    pair3_ref,
    wt,
    weights,
    wb,
    turned_wb,
    values,
    hi,
    lo,
    row_out,
    pair_sum,
    pair_out,
):
    step = pl.program_id(0)
    heads, rows, columns = scores_ref.shape
    group, width, _ = att_ref.shape
    dim = width // heads
    wide = col_ref.shape[2]

    @pl.when(step == 0)
    def _():
        wt[...] = turned(payload_ref[...])
        pair_sum[...] = jnp.zeros(pair_sum.shape, F32)
        peaks = stats_ref[:, 0:heads]
        peak = jnp.max(peaks, axis=0)
        total = jnp.sum(stats_ref[:, heads : 2 * heads] * jnp.exp(peaks - peak[None]), axis=0)
        table = jnp.concatenate([peak, 1.0 / total, jnp.zeros((128 - 2 * heads, rows), F32)], axis=0).T
        keep = keep_ref[...] > 0
        for h in range(heads):
            masked = jnp.where(keep, scores_ref[h], MASKED)
            exact = jnp.exp(masked - table[:, h : h + 1]) * table[:, heads + h : heads + h + 1]
            weights[h] = exact
            wb[h] = exact.astype(BF16)
            turned_wb[h] = exact.T.astype(BF16)

    first = pl.multiple_of(step * group, group)
    for h in range(heads):
        block = att_ref[:, h * dim : (h + 1) * dim, :].reshape(group * dim, rows)
        split(dot(block, wb[h]).reshape(group, dim, columns), hi, lo, h, dim)
    project_rows(payload_ref[...], hi, lo, col_ref, first)

    own = place_ref[0] == place_ref[1]
    tokens = jnp.where(own, mine_ref[pl.ds(first, group)], other_ref[pl.ds(first, group)])
    for k in range(group):
        values[k] = dot(wt[...], tokens[k]).astype(BF16)
    for h in range(heads):
        block = values[:, h * dim : (h + 1) * dim, :].reshape(group * dim, columns)
        average = dot(block, turned_wb[h]).reshape(group, dim, rows)
        split(average * term_ref[:, h * dim : (h + 1) * dim, :].astype(F32), hi, lo, h, dim)
        pair_sum[h] += dot(att_rows_ref[h], block)
    project_rows(gate_w_ref[...], hi, lo, row_out, first)

    @pl.when(step == pl.num_programs(0) - 1)
    def _():
        lane = lax.broadcasted_iota(jnp.int32, (rows, 128), 1)
        table = jnp.zeros((rows, 128), F32)
        owners = pair_out.shape[0]
        own_heads = heads // owners
        for k in range(owners):
            tails = []
            for g in range(own_heads):
                h = k * own_heads + g
                grad = pair_sum[h].astype(BF16)
                pair_out[k, g] = grad[:, 0:128]
                tails.append(grad[:, 128:192])
                inner = jnp.sum(weights[h] * grad.astype(F32), axis=1, keepdims=True)
                table = jnp.where(lane == h, inner, table)
            pair_out[k, own_heads] = jnp.concatenate(tails, axis=-1)
        inner = thirds(jnp.concatenate([table.T[0:heads], jnp.zeros((heads, 256 - rows), F32)], axis=-1))
        for k, out_ref in enumerate((row0_ref, row1_ref, row2_ref, row3_ref)):
            out_ref[:, :, 0:wide] = row_out[pl.ds(2 * (place_ref[2] ^ k), 2)]
            for z in range(2):
                out_ref[z, :, wide:] = inner
        for k, out_ref in enumerate((pair0_ref, pair1_ref, pair2_ref, pair3_ref)):
            out_ref[...] = pair_out[place_ref[3] ^ k]
        weights_ref[...] = weights[pl.ds(place_ref[3] * own_heads, own_heads)]


def score_kernel(
    place_ref,
    part0_ref,
    part1_ref,
    part2_ref,
    part3_ref,
    inner0_ref,
    inner1_ref,
    inner2_ref,
    inner3_ref,
    weights_ref,
    out_ref,
):
    heads, rows, _ = out_ref.shape
    total = part0_ref[...].astype(F32)
    for part in (part1_ref, part2_ref, part3_ref):
        total = total + part[...].astype(F32)
    inner = ((inner0_ref[...] + inner1_ref[...]) + (inner2_ref[...] + inner3_ref[...]))[:, 0:rows]
    table = jnp.concatenate([inner, jnp.zeros((128 - inner.shape[0], rows), F32)], axis=0).T
    lane = lax.broadcasted_iota(jnp.int32, table.shape, 1)
    for h in range(heads):
        mine = place_ref[3] * heads + h
        grad = jnp.concatenate([total[h], total[heads][:, 64 * h : 64 * h + 64]], axis=-1)
        own = jnp.sum(jnp.where(lane == mine, table, 0.0), axis=1, keepdims=True)
        out_ref[h] = weights_ref[h] * (grad - own)


def fold_kernel(place_ref, part0_ref, part1_ref, part2_ref, part3_ref, keep_ref, inner_ref, send_ref):
    wide = keep_ref.shape[1]
    parts = (part0_ref, part1_ref, part2_ref, part3_ref)
    total = sum(part[:, :, 0:wide].astype(F32) for part in parts)
    high = place_ref[1] == 1
    keep_ref[...] = jnp.where(high, total[1], total[0])
    send_ref[:, 0:wide] = jnp.where(high, total[0], total[1]).astype(BF16)
    inner = sum(joined(part[0, :, wide:]) for part in parts)
    inner_ref[...] = inner
    send_ref[:, wide:] = thirds(inner)


def inner_kernel(inner_ref, rows_ref, out_ref):
    out_ref[...] = inner_ref[...] + joined(rows_ref[:, rows_ref.shape[1] - 256 :])


def join_kernel(keep_ref, rows_ref, cols_ref, out_ref):
    sequences, _, features = out_ref.shape
    total = keep_ref[...] + rows_ref[:, 0 : keep_ref.shape[1]].astype(F32) + cols_ref[...].astype(F32)
    for s in range(sequences):
        out_ref[s] = total[:, s * features : (s + 1) * features]


def body(
    layernormed_alignment,
    average_cotangent,
    sequence_validity,
    residue_validity,
    pair_scores,
    payload_projection,
    sigmoid_projection,
    final_projection,
):
    row_count = lax.axis_size("row")
    col_count = lax.axis_size("col")
    seq_count = lax.axis_size("seq")
    row_pos = lax.axis_index("row")
    col_pos = lax.axis_index("col")
    seq_pos = lax.axis_index("seq")
    sequences, rows, features = layernormed_alignment.shape
    heads, _, columns = pair_scores.shape
    width = payload_projection.shape[1]
    dim = width // heads
    stretch = rows // col_count
    wide = sequences * features
    own = heads // seq_count
    group = sequences // STEPS
    side = row_count // 2
    core, plane, across = row_pos % 2, col_pos % 2, col_pos // 2
    place = jnp.stack([core, plane, across, seq_pos]).astype(jnp.int32)

    tokens = far(jnp.swapaxes(layernormed_alignment, 1, 2))
    cotangent = far(jnp.swapaxes(average_cotangent, 1, 2))
    scores = far(pair_scores)
    payload_w = far(payload_projection)
    gate_w = far(sigmoid_projection)
    final_w = far(final_projection.T)
    keep = lax.dynamic_slice_in_dim(residue_validity, col_pos * columns, columns, 0).reshape(1, columns)

    at = lambda x, core, y, z: (x * 2 + core) * col_count + y * 2 + z
    routes = [
        (at(a, z, b, z), at((b + 2 * a) % side, z, a, z))
        for a in range(side)
        for b in range(side)
        for z in range(2)
    ]
    mine = lax.ppermute(jnp.swapaxes(layernormed_alignment, 1, 2), ("row", "col"), routes)

    stats = call(
        stats_kernel,
        jax.ShapeDtypeStruct((col_count, 2 * heads, rows), F32),
        [scores, keep],
        moved=4 << 20,
    )
    stats = lax.all_to_all(stats, "col", 0, 0, tiled=True)

    by_lanes = pl.BlockSpec((heads, rows, group * dim), lambda i: (0, 0, i))
    d_att, gate_term, att_rows = call(
        gate_kernel,
        [
            pltpu.HBM((sequences, width, rows), BF16),
            pltpu.HBM((sequences, width, rows), BF16),
            pltpu.HBM((heads, rows, sequences * dim), BF16),
        ],
        [tokens, cotangent, far(sequence_validity), gate_w, final_w],
        [
            by_step(group, features, rows),
            by_step(group, features, rows),
            by_step(group, rows),
            whole((features, width)),
            whole((features, width)),
        ],
        [by_step(group, width, rows), by_step(group, width, rows), by_lanes],
        grid=(STEPS,),
        scratch=[pltpu.VMEM((2, width, features), BF16)],
        flops=1 << 30,
        moved=14 << 20,
    )
    mine, stats, d_att = lax.optimization_barrier((mine, stats, d_att))
    other = lax.ppermute(mine, "row", [(i, i ^ 1) for i in range(row_count)])

    message = wide + 256
    pieces = pltpu.VMEM((group, width, rows), BF16)
    square = pltpu.VMEM((heads, rows, columns), F32)
    weights, col_term, *sent = call(
        main_kernel,
        [jax.ShapeDtypeStruct((own, rows, columns), F32), jax.ShapeDtypeStruct((row_count, stretch, wide), BF16)]
        + [jax.ShapeDtypeStruct((2, stretch, message), BF16)] * side
        + [jax.ShapeDtypeStruct((own + 1, rows, 128), BF16)] * seq_count,
        [scores, keep, stats, far(d_att), far(gate_term), far(att_rows), mine, other, payload_w, gate_w],
        [
            whole((heads, rows, columns)),
            whole((1, columns)),
            whole((col_count, 2 * heads, rows)),
            by_step(group, width, rows),
            by_step(group, width, rows),
            by_lanes,
            whole((sequences, features, rows)),
            whole((sequences, features, rows)),
            whole((features, width)),
            whole((features, width)),
        ],
        [whole((own, rows, columns)), whole((row_count, stretch, wide))]
        + [whole((2, stretch, message)) for _ in range(side)]
        + [whole((own + 1, rows, 128)) for _ in range(seq_count)],
        grid=(STEPS,),
        scratch=[
            pltpu.VMEM((width, features), BF16),
            square,
            pltpu.VMEM((heads, rows, columns), BF16),
            pltpu.VMEM((heads, columns, rows), BF16),
            pieces,
            pieces,
            pieces,
            pltpu.VMEM((col_count, stretch, wide), BF16),
            square,
            pltpu.VMEM((seq_count, own + 1, rows, 128), BF16),
        ],
        scalars=place,
        flops=1 << 30,
        moved=18 << 20,
    )
    row_term, d_weights = sent[:side], sent[side:]

    def swapped(a, axis, bits):
        return lax.ppermute(a, axis, [(i, i ^ bits) for i in range(lax.axis_size(axis))])

    row_term = row_term[:1] + [swapped(row_term[k], "col", 2 * k) for k in range(1, side)]
    d_weights = d_weights[:1] + [swapped(d_weights[k], "seq", k) for k in range(1, seq_count)]
    col_term = lax.all_to_all(col_term, "row", 0, 0, tiled=True)
    col_term = jnp.sum(col_term.astype(F32), axis=0).astype(BF16)
    col_term = lax.ppermute(
        col_term,
        ("row", "col"),
        [(r * col_count + c, c * col_count + r) for r in range(row_count) for c in range(col_count)],
    )
    row_keep, inner, row_send = call(
        fold_kernel,
        [
            jax.ShapeDtypeStruct((stretch, wide), F32),
            jax.ShapeDtypeStruct((heads, 256), F32),
            jax.ShapeDtypeStruct((stretch, message), BF16),
        ],
        row_term,
        scalars=place,
        moved=2 << 20,
    )
    row_send = swapped(row_send, "col", 1)
    inner = call(inner_kernel, jax.ShapeDtypeStruct((heads, 256), F32), [inner, row_send], moved=1 << 20)
    inners = [inner] + [swapped(inner, "seq", k) for k in range(1, seq_count)]
    score_cotangent = call(
        score_kernel,
        jax.ShapeDtypeStruct((own, rows, columns), F32),
        d_weights + inners + [weights],
        scalars=place,
        moved=2 << 20,
    )
    alignment_cotangent = call(
        join_kernel,
        jax.ShapeDtypeStruct((sequences, stretch, features), F32),
        [row_keep, row_send, col_term],
        moved=2 << 20,
    )
    return (alignment_cotangent, score_cotangent)


def solution(mesh):
    return jax.shard_map(
        body,
        mesh=mesh,
        in_specs=(
            P("seq", "row", None),
            P("seq", "row", None),
            P("seq", "row"),
            P(),
            P(None, "row", "col"),
            P(),
            P(),
            P(),
        ),
        out_specs=(P("seq", ("row", "col"), None), P("seq", "row", "col")),
        check_vma=False,
    )
```

```python
import jax
import jax.numpy as jnp
from jax import lax
from jax.experimental import pallas as pl
from jax.experimental.pallas import tpu as pltpu
from jax.sharding import PartitionSpec as P

F32 = jnp.float32
BF16 = jnp.bfloat16
MASKED = -1000000000.0
VMEM_BYTES = 24 * 1024 * 1024
STEPS = 4


def call(kernel, outs, inputs, in_specs=None, out_specs=None, grid=None, scratch=(), scalars=None, flops=0, moved=0):
    local = lambda: pl.BlockSpec(memory_space=pltpu.VMEM)
    several = isinstance(outs, list)
    operands = [] if scalars is None else [scalars]
    if in_specs is None:
        in_specs = [local() for _ in inputs]
    if out_specs is None:
        out_specs = [local() for _ in outs] if several else local()
    extra = {} if grid is None else {"grid": grid}
    return pl.pallas_call(
        kernel,
        out_shape=outs,
        in_specs=[pl.BlockSpec(memory_space=pltpu.SMEM)] * len(operands) + in_specs,
        out_specs=out_specs,
        scratch_shapes=list(scratch),
        compiler_params=pltpu.CompilerParams(vmem_limit_bytes=VMEM_BYTES),
        cost_estimate=pl.CostEstimate(flops=flops, bytes_accessed=moved, transcendentals=0),
        **extra,
    )(*operands, *inputs)


def whole(shape):
    return pl.BlockSpec(shape, lambda i: (0,) * len(shape))


def by_step(*dims):
    return pl.BlockSpec(dims, lambda i: (i,) + (0,) * (len(dims) - 1))


def far(a):
    return pltpu.with_memory_space_constraint(a, pltpu.HBM)


def dot(a, b):
    return jnp.dot(a, b, preferred_element_type=F32)


def turned(a):
    return a.astype(F32).T.astype(a.dtype)


def stats_kernel(scores_ref, keep_ref, stats_ref):
    heads, rows, _ = scores_ref.shape
    keep = keep_ref[...] > 0
    lane = lax.broadcasted_iota(jnp.int32, (rows, 128), 1)
    table = jnp.zeros((rows, 128), F32)
    for h in range(heads):
        masked = jnp.where(keep, scores_ref[h], MASKED)
        peak = jnp.max(masked, axis=1, keepdims=True)
        total = jnp.sum(jnp.exp(masked - peak), axis=1, keepdims=True)
        table = jnp.where(lane == h, peak, table)
        table = jnp.where(lane == heads + h, total, table)
    packed = table.T[0 : 2 * heads]
    for k in range(stats_ref.shape[0]):
        stats_ref[k] = packed


def project_rows(weight, pieces, out_ref, first):
    sequences = pieces.shape[0]
    chunks, stretch, _ = out_ref.shape
    features = weight.shape[0]
    for s in range(0, sequences, 2):
        pair = [dot(weight, pieces[s + k]) for k in (0, 1)]
        rows = jnp.concatenate(pair, axis=0).T.reshape(chunks, stretch, 2 * features)
        lanes = pl.ds(pl.multiple_of((first + s) * features, 128), 2 * features)
        out_ref[:, :, lanes] = rows.astype(out_ref.dtype)


def thirds(table):
    first = table.astype(BF16)
    rest = table - first.astype(F32)
    second = rest.astype(BF16)
    third = (rest - second.astype(F32)).astype(BF16)
    return jnp.concatenate([t.astype(F32) for t in (first, second, third)], axis=0).astype(BF16)


def joined(table):
    count = table.shape[0] // 3
    table = table.astype(F32)
    return table[0:count] + table[count : 2 * count] + table[2 * count : 3 * count]


def main_kernel(
    place_ref,
    scores_ref,
    keep_ref,
    stats_ref,
    x_ref,
    cot_ref,
    mask_ref,
    mine_ref,
    other_ref,
    payload_ref,
    gate_w_ref,
    final_w_ref,
    weights_ref,
    col_ref,
    row0_ref,
    row1_ref,
    row2_ref,
    row3_ref,
    pair0_ref,
    pair1_ref,
    pair2_ref,
    pair3_ref,
    wt,
    weights,
    wb,
    turned_wb,
    att,
    term,
    values,
    pieces,
    row_out,
    pair_sum,
    pair_out,
):
    step = pl.program_id(0)
    heads, rows, columns = scores_ref.shape
    group = x_ref.shape[0]
    width = payload_ref.shape[1]
    dim = width // heads
    wide = col_ref.shape[2]

    @pl.when(step == 0)
    def _():
        for k, weight in enumerate((payload_ref, gate_w_ref, final_w_ref)):
            wt[k] = turned(weight[...])
        pair_sum[...] = jnp.zeros(pair_sum.shape, F32)
        peaks = stats_ref[:, 0:heads]
        peak = jnp.max(peaks, axis=0)
        total = jnp.sum(stats_ref[:, heads : 2 * heads] * jnp.exp(peaks - peak[None]), axis=0)
        table = jnp.concatenate([peak, 1.0 / total, jnp.zeros((128 - 2 * heads, rows), F32)], axis=0).T
        keep = keep_ref[...] > 0
        for h in range(heads):
            masked = jnp.where(keep, scores_ref[h], MASKED)
            exact = jnp.exp(masked - table[:, h : h + 1]) * table[:, heads + h : heads + h + 1]
            weights[h] = exact
            wb[h] = exact.astype(BF16)
            turned_wb[h] = exact.T.astype(BF16)

    first = pl.multiple_of(step * group, group)
    mask = mask_ref[...].astype(F32)
    for k in range(group):
        gate = 1.0 / (1.0 + jnp.exp(-dot(wt[1], x_ref[k])))
        cot = dot(wt[2], cot_ref[k]) * mask[k : k + 1]
        exact = cot * gate
        att[k] = exact.astype(BF16)
        term[k] = exact * (1.0 - gate)
    for h in range(heads):
        block = att[:, h * dim : (h + 1) * dim, :].reshape(group * dim, rows)
        pieces[:, h * dim : (h + 1) * dim, :] = dot(block, wb[h]).astype(BF16).reshape(group, dim, columns)
    project_rows(payload_ref[...], pieces, col_ref, first)

    own = place_ref[0] != place_ref[1]
    tokens = jnp.where(own, mine_ref[pl.ds(first, group)], other_ref[pl.ds(first, group)])
    for k in range(group):
        values[k] = dot(wt[0], tokens[k]).astype(BF16)
    for h in range(heads):
        block = values[:, h * dim : (h + 1) * dim, :].reshape(group * dim, columns)
        average = dot(block, turned_wb[h]).reshape(group, dim, rows)
        pieces[:, h * dim : (h + 1) * dim, :] = (average * term[:, h * dim : (h + 1) * dim, :]).astype(BF16)
        att_rows = turned(att[:, h * dim : (h + 1) * dim, :].reshape(group * dim, rows))
        pair_sum[h] += dot(att_rows, block)
    project_rows(gate_w_ref[...], pieces, row_out, first)

    @pl.when(step == pl.num_programs(0) - 1)
    def _():
        lane = lax.broadcasted_iota(jnp.int32, (rows, 128), 1)
        table = jnp.zeros((rows, 128), F32)
        owners = pair_out.shape[0]
        own_heads = heads // owners
        for k in range(owners):
            tails = []
            for g in range(own_heads):
                h = k * own_heads + g
                grad = pair_sum[h].astype(BF16)
                pair_out[k, g] = grad[:, 0:128]
                tails.append(grad[:, 128:192])
                inner = jnp.sum(weights[h] * grad.astype(F32), axis=1, keepdims=True)
                table = jnp.where(lane == h, inner, table)
            pair_out[k, own_heads] = jnp.concatenate(tails, axis=-1)
        inner = thirds(jnp.concatenate([table.T[0:heads], jnp.zeros((heads, 256 - rows), F32)], axis=-1))
        for k, out_ref in enumerate((row0_ref, row1_ref, row2_ref, row3_ref)):
            out_ref[:, :, 0:wide] = row_out[pl.ds(2 * (place_ref[2] ^ k), 2)]
            for z in range(2):
                out_ref[z, :, wide:] = inner
        for k, out_ref in enumerate((pair0_ref, pair1_ref, pair2_ref, pair3_ref)):
            out_ref[...] = pair_out[place_ref[3] ^ k]
        weights_ref[...] = weights[pl.ds(place_ref[3] * own_heads, own_heads)]


def score_kernel(
    place_ref,
    part0_ref,
    part1_ref,
    part2_ref,
    part3_ref,
    inner0_ref,
    inner1_ref,
    inner2_ref,
    inner3_ref,
    weights_ref,
    out_ref,
):
    heads, rows, _ = out_ref.shape
    total = part0_ref[...].astype(F32)
    for part in (part1_ref, part2_ref, part3_ref):
        total = total + part[...].astype(F32)
    inner = ((inner0_ref[...] + inner1_ref[...]) + (inner2_ref[...] + inner3_ref[...]))[:, 0:rows]
    table = jnp.concatenate([inner, jnp.zeros((128 - inner.shape[0], rows), F32)], axis=0).T
    lane = lax.broadcasted_iota(jnp.int32, table.shape, 1)
    for h in range(heads):
        mine = place_ref[3] * heads + h
        grad = jnp.concatenate([total[h], total[heads][:, 64 * h : 64 * h + 64]], axis=-1)
        own = jnp.sum(jnp.where(lane == mine, table, 0.0), axis=1, keepdims=True)
        out_ref[h] = weights_ref[h] * (grad - own)


def fold_kernel(place_ref, part0_ref, part1_ref, part2_ref, part3_ref, keep_ref, inner_ref, send_ref):
    wide = keep_ref.shape[1]
    parts = (part0_ref, part1_ref, part2_ref, part3_ref)
    total = sum(part[:, :, 0:wide].astype(F32) for part in parts)
    high = place_ref[1] == 1
    keep_ref[...] = jnp.where(high, total[1], total[0])
    send_ref[:, 0:wide] = jnp.where(high, total[0], total[1]).astype(BF16)
    inner = sum(joined(part[0, :, wide:]) for part in parts)
    inner_ref[...] = inner
    send_ref[:, wide:] = thirds(inner)


def inner_kernel(inner_ref, rows_ref, out_ref):
    out_ref[...] = inner_ref[...] + joined(rows_ref[:, rows_ref.shape[1] - 256 :])


def join_kernel(keep_ref, rows_ref, cols_ref, out_ref):
    sequences, _, features = out_ref.shape
    total = keep_ref[...] + rows_ref[:, 0 : keep_ref.shape[1]].astype(F32) + cols_ref[...].astype(F32)
    for s in range(sequences):
        out_ref[s] = total[:, s * features : (s + 1) * features]


def body(
    layernormed_alignment,
    average_cotangent,
    sequence_validity,
    residue_validity,
    pair_scores,
    payload_projection,
    sigmoid_projection,
    final_projection,
):
    row_count = lax.axis_size("row")
    col_count = lax.axis_size("col")
    seq_count = lax.axis_size("seq")
    row_pos = lax.axis_index("row")
    col_pos = lax.axis_index("col")
    seq_pos = lax.axis_index("seq")
    sequences, rows, features = layernormed_alignment.shape
    heads, _, columns = pair_scores.shape
    width = payload_projection.shape[1]
    dim = width // heads
    stretch = rows // col_count
    wide = sequences * features
    own = heads // seq_count
    group = sequences // STEPS
    side = row_count // 2
    core, plane, across = row_pos % 2, col_pos % 2, col_pos // 2
    place = jnp.stack([core, plane, across, seq_pos]).astype(jnp.int32)

    tokens = far(jnp.swapaxes(layernormed_alignment, 1, 2))
    cotangent = far(jnp.swapaxes(average_cotangent, 1, 2))
    scores = far(pair_scores)
    payload_w = far(payload_projection)
    gate_w = far(sigmoid_projection)
    final_w = far(final_projection.T)
    keep = lax.dynamic_slice_in_dim(residue_validity, col_pos * columns, columns, 0).reshape(1, columns)

    at = lambda x, core, y, z: (x * 2 + core) * col_count + y * 2 + z
    routes = [
        (at(a, z, b, z), at((b + 2 * a) % side, 1 - z, a, z))
        for a in range(side)
        for b in range(side)
        for z in range(2)
    ]
    mine = lax.ppermute(jnp.swapaxes(layernormed_alignment, 1, 2), ("row", "col"), routes)

    local_stats = call(
        stats_kernel,
        jax.ShapeDtypeStruct((col_count, 2 * heads, rows), F32),
        [scores, keep],
        moved=4 << 20,
    )
    stats = lax.all_to_all(local_stats, "col", 0, 0, tiled=True)

    mine, stats = lax.optimization_barrier((mine, stats))
    other = lax.ppermute(mine, "row", [(i, i ^ 1) for i in range(row_count)])

    message = wide + 256
    pieces = pltpu.VMEM((group, width, rows), BF16)
    square = pltpu.VMEM((heads, rows, columns), F32)
    weights, col_term, *sent = call(
        main_kernel,
        [jax.ShapeDtypeStruct((own, rows, columns), F32), jax.ShapeDtypeStruct((row_count, stretch, wide), BF16)]
        + [jax.ShapeDtypeStruct((2, stretch, message), BF16)]
        + [pltpu.HBM((2, stretch, message), BF16)] * (side - 1)
        + [jax.ShapeDtypeStruct((own + 1, rows, 128), BF16)] * seq_count,
        [scores, keep, stats, tokens, cotangent, far(sequence_validity), mine, other, payload_w, gate_w, final_w],
        [
            whole((heads, rows, columns)),
            whole((1, columns)),
            whole((col_count, 2 * heads, rows)),
            by_step(group, features, rows),
            by_step(group, features, rows),
            by_step(group, rows),
            whole((sequences, features, rows)),
            whole((sequences, features, rows)),
            whole((features, width)),
            whole((features, width)),
            whole((features, width)),
        ],
        [whole((own, rows, columns)), whole((row_count, stretch, wide))]
        + [whole((2, stretch, message)) for _ in range(side)]
        + [whole((own + 1, rows, 128)) for _ in range(seq_count)],
        grid=(STEPS,),
        scratch=[
            pltpu.VMEM((3, width, features), BF16),
            square,
            pltpu.VMEM((heads, rows, columns), BF16),
            pltpu.VMEM((heads, columns, rows), BF16),
            pieces,
            pltpu.VMEM((group, width, rows), F32),
            pieces,
            pieces,
            pltpu.VMEM((col_count, stretch, wide), BF16),
            square,
            pltpu.VMEM((seq_count, own + 1, rows, 128), BF16),
        ],
        scalars=place,
        flops=1 << 30,
        moved=18 << 20,
    )
    row_term, d_weights = sent[:side], sent[side:]

    def swapped(a, axis, bits):
        return lax.ppermute(a, axis, [(i, i ^ bits) for i in range(lax.axis_size(axis))])

    row_term = row_term[:1] + [swapped(row_term[k], "col", 2 * k) for k in range(1, side)]
    d_weights = d_weights[:1] + [swapped(d_weights[k], "seq", k) for k in range(1, seq_count)]
    col_term = lax.all_to_all(col_term, "row", 0, 0, tiled=True)
    col_term = jnp.sum(col_term.astype(F32), axis=0).astype(BF16)
    col_term = lax.ppermute(
        col_term,
        ("row", "col"),
        [(r * col_count + c, c * col_count + r) for r in range(row_count) for c in range(col_count)],
    )
    row_keep, inner, row_send = call(
        fold_kernel,
        [
            jax.ShapeDtypeStruct((stretch, wide), F32),
            jax.ShapeDtypeStruct((heads, 256), F32),
            jax.ShapeDtypeStruct((stretch, message), BF16),
        ],
        row_term,
        scalars=place,
        moved=2 << 20,
    )
    row_send = swapped(row_send, "col", 1)
    inner = call(inner_kernel, jax.ShapeDtypeStruct((heads, 256), F32), [inner, row_send], moved=1 << 20)
    inners = [inner] + [swapped(inner, "seq", k) for k in range(1, seq_count)]
    score_cotangent = call(
        score_kernel,
        jax.ShapeDtypeStruct((own, rows, columns), F32),
        d_weights + inners + [weights],
        scalars=place,
        moved=2 << 20,
    )
    alignment_cotangent = call(
        join_kernel,
        jax.ShapeDtypeStruct((sequences, stretch, features), F32),
        [row_keep, row_send, col_term],
        moved=2 << 20,
    )
    return (alignment_cotangent, score_cotangent)


def solution(mesh):
    return jax.shard_map(
        body,
        mesh=mesh,
        in_specs=(
            P("seq", "row", None),
            P("seq", "row", None),
            P("seq", "row"),
            P(),
            P(None, "row", "col"),
            P(),
            P(),
            P(),
        ),
        out_specs=(P("seq", ("row", "col"), None), P("seq", "row", "col")),
        check_vma=False,
    )
```

```python
import jax
import jax.numpy as jnp
from jax import lax
from jax.experimental import pallas as pl
from jax.experimental.pallas import tpu as pltpu
from jax.sharding import PartitionSpec as P

F32 = jnp.float32
BF16 = jnp.bfloat16
MASKED = -1000000000.0
VMEM_BYTES = 24 * 1024 * 1024
STEPS = 2


def call(kernel, outs, inputs, in_specs=None, out_specs=None, grid=None, scratch=(), scalars=None, flops=0, moved=0):
    local = lambda: pl.BlockSpec(memory_space=pltpu.VMEM)
    several = isinstance(outs, list)
    operands = [] if scalars is None else [scalars]
    if in_specs is None:
        in_specs = [local() for _ in inputs]
    if out_specs is None:
        out_specs = [local() for _ in outs] if several else local()
    extra = {} if grid is None else {"grid": grid}
    return pl.pallas_call(
        kernel,
        out_shape=outs,
        in_specs=[pl.BlockSpec(memory_space=pltpu.SMEM)] * len(operands) + in_specs,
        out_specs=out_specs,
        scratch_shapes=list(scratch),
        compiler_params=pltpu.CompilerParams(vmem_limit_bytes=VMEM_BYTES),
        cost_estimate=pl.CostEstimate(flops=flops, bytes_accessed=moved, transcendentals=0),
        **extra,
    )(*operands, *inputs)


def whole(shape):
    return pl.BlockSpec(shape, lambda i: (0,) * len(shape))


def by_step(*dims):
    return pl.BlockSpec(dims, lambda i: (i,) + (0,) * (len(dims) - 1))


def far(a):
    return pltpu.with_memory_space_constraint(a, pltpu.HBM)


def dot(a, b):
    return jnp.dot(a, b, preferred_element_type=F32)


def turned(a):
    return a.astype(F32).T.astype(a.dtype)


def stats_kernel(scores_ref, keep_ref, stats_ref):
    heads, rows, _ = scores_ref.shape
    keep = keep_ref[...] > 0
    lane = lax.broadcasted_iota(jnp.int32, (rows, 128), 1)
    table = jnp.zeros((rows, 128), F32)
    for h in range(heads):
        masked = jnp.where(keep, scores_ref[h], MASKED)
        peak = jnp.max(masked, axis=1, keepdims=True)
        total = jnp.sum(jnp.exp(masked - peak), axis=1, keepdims=True)
        table = jnp.where(lane == h, peak, table)
        table = jnp.where(lane == heads + h, total, table)
    packed = table.T[0 : 2 * heads]
    for k in range(stats_ref.shape[0]):
        stats_ref[k] = packed


def project_rows(weight, pieces, out_ref, first):
    sequences = pieces.shape[0]
    chunks, stretch, _ = out_ref.shape
    features = weight.shape[0]
    for s in range(0, sequences, 2):
        pair = [dot(weight, pieces[s + k]) for k in (0, 1)]
        rows = jnp.concatenate(pair, axis=0).T.reshape(chunks, stretch, 2 * features)
        lanes = pl.ds(pl.multiple_of((first + s) * features, 128), 2 * features)
        out_ref[:, :, lanes] = rows.astype(out_ref.dtype)


def thirds(table):
    first = table.astype(BF16)
    rest = table - first.astype(F32)
    second = rest.astype(BF16)
    third = (rest - second.astype(F32)).astype(BF16)
    return jnp.concatenate([t.astype(F32) for t in (first, second, third)], axis=0).astype(BF16)


def joined(table):
    count = table.shape[0] // 3
    table = table.astype(F32)
    return table[0:count] + table[count : 2 * count] + table[2 * count : 3 * count]


def main_kernel(
    place_ref,
    scores_ref,
    keep_ref,
    stats_ref,
    x_ref,
    cot_ref,
    mask_ref,
    mine_ref,
    other_ref,
    payload_ref,
    gate_w_ref,
    final_w_ref,
    weights_ref,
    col_ref,
    row0_ref,
    row1_ref,
    row2_ref,
    row3_ref,
    pair0_ref,
    pair1_ref,
    pair2_ref,
    pair3_ref,
    wt,
    weights,
    wb,
    turned_wb,
    att,
    term,
    values,
    pieces,
    row_out,
    pair_sum,
    pair_out,
):
    step = pl.program_id(0)
    heads, rows, columns = scores_ref.shape
    group = x_ref.shape[0]
    width = payload_ref.shape[1]
    dim = width // heads
    wide = col_ref.shape[2]

    @pl.when(step == 0)
    def _():
        for k, weight in enumerate((payload_ref, gate_w_ref, final_w_ref)):
            wt[k] = turned(weight[...])
        pair_sum[...] = jnp.zeros(pair_sum.shape, F32)
        peaks = stats_ref[:, 0:heads]
        peak = jnp.max(peaks, axis=0)
        total = jnp.sum(stats_ref[:, heads : 2 * heads] * jnp.exp(peaks - peak[None]), axis=0)
        table = jnp.concatenate([peak, 1.0 / total, jnp.zeros((128 - 2 * heads, rows), F32)], axis=0).T
        keep = keep_ref[...] > 0
        for h in range(heads):
            masked = jnp.where(keep, scores_ref[h], MASKED)
            exact = jnp.exp(masked - table[:, h : h + 1]) * table[:, heads + h : heads + h + 1]
            weights[h] = exact
            wb[h] = exact.astype(BF16)
            turned_wb[h] = exact.T.astype(BF16)

    first = pl.multiple_of(step * group, group)
    mask = mask_ref[...].astype(F32)
    for k in range(group):
        gate = 1.0 / (1.0 + jnp.exp(-dot(wt[1], x_ref[k])))
        cot = dot(wt[2], cot_ref[k]) * mask[k : k + 1]
        exact = cot * gate
        att[k] = exact.astype(BF16)
        term[k] = exact * (1.0 - gate)
    for h in range(heads):
        block = att[:, h * dim : (h + 1) * dim, :].reshape(group * dim, rows)
        pieces[:, h * dim : (h + 1) * dim, :] = dot(block, wb[h]).astype(BF16).reshape(group, dim, columns)
    project_rows(payload_ref[...], pieces, col_ref, first)

    own = place_ref[0] != place_ref[1]
    tokens = jnp.where(own, mine_ref[pl.ds(first, group)], other_ref[pl.ds(first, group)])
    for k in range(group):
        values[k] = dot(wt[0], tokens[k]).astype(BF16)
    for h in range(heads):
        block = values[:, h * dim : (h + 1) * dim, :].reshape(group * dim, columns)
        average = dot(block, turned_wb[h]).reshape(group, dim, rows)
        pieces[:, h * dim : (h + 1) * dim, :] = (average * term[:, h * dim : (h + 1) * dim, :]).astype(BF16)
        att_rows = turned(att[:, h * dim : (h + 1) * dim, :].reshape(group * dim, rows))
        pair_sum[h] += dot(att_rows, block)
    project_rows(gate_w_ref[...], pieces, row_out, first)

    @pl.when(step == pl.num_programs(0) - 1)
    def _():
        lane = lax.broadcasted_iota(jnp.int32, (rows, 128), 1)
        table = jnp.zeros((rows, 128), F32)
        owners = pair_out.shape[0]
        own_heads = heads // owners
        for k in range(owners):
            tails = []
            for g in range(own_heads):
                h = k * own_heads + g
                grad = pair_sum[h].astype(BF16)
                pair_out[k, g] = grad[:, 0:128]
                tails.append(grad[:, 128:192])
                inner = jnp.sum(weights[h] * grad.astype(F32), axis=1, keepdims=True)
                table = jnp.where(lane == h, inner, table)
            pair_out[k, own_heads] = jnp.concatenate(tails, axis=-1)
        inner = thirds(jnp.concatenate([table.T[0:heads], jnp.zeros((heads, 256 - rows), F32)], axis=-1))
        for k, out_ref in enumerate((row0_ref, row1_ref, row2_ref, row3_ref)):
            out_ref[:, :, 0:wide] = row_out[pl.ds(2 * (place_ref[2] ^ k), 2)]
            for z in range(2):
                out_ref[z, :, wide:] = inner
        for k, out_ref in enumerate((pair0_ref, pair1_ref, pair2_ref, pair3_ref)):
            out_ref[...] = pair_out[place_ref[3] ^ k]
        weights_ref[...] = weights[pl.ds(place_ref[3] * own_heads, own_heads)]


def score_kernel(
    place_ref,
    part0_ref,
    part1_ref,
    part2_ref,
    part3_ref,
    inner0_ref,
    inner1_ref,
    inner2_ref,
    inner3_ref,
    weights_ref,
    out_ref,
):
    heads, rows, _ = out_ref.shape
    total = part0_ref[...].astype(F32)
    for part in (part1_ref, part2_ref, part3_ref):
        total = total + part[...].astype(F32)
    inner = ((inner0_ref[...] + inner1_ref[...]) + (inner2_ref[...] + inner3_ref[...]))[:, 0:rows]
    table = jnp.concatenate([inner, jnp.zeros((128 - inner.shape[0], rows), F32)], axis=0).T
    lane = lax.broadcasted_iota(jnp.int32, table.shape, 1)
    for h in range(heads):
        mine = place_ref[3] * heads + h
        grad = jnp.concatenate([total[h], total[heads][:, 64 * h : 64 * h + 64]], axis=-1)
        own = jnp.sum(jnp.where(lane == mine, table, 0.0), axis=1, keepdims=True)
        out_ref[h] = weights_ref[h] * (grad - own)


def fold_kernel(place_ref, part0_ref, part1_ref, part2_ref, part3_ref, keep_ref, inner_ref, send_ref):
    wide = keep_ref.shape[1]
    parts = (part0_ref, part1_ref, part2_ref, part3_ref)
    total = sum(part[:, :, 0:wide].astype(F32) for part in parts)
    high = place_ref[1] == 1
    keep_ref[...] = jnp.where(high, total[1], total[0])
    send_ref[:, 0:wide] = jnp.where(high, total[0], total[1]).astype(BF16)
    inner = sum(joined(part[0, :, wide:]) for part in parts)
    inner_ref[...] = inner
    send_ref[:, wide:] = thirds(inner)


def inner_kernel(inner_ref, rows_ref, out_ref):
    out_ref[...] = inner_ref[...] + joined(rows_ref[:, rows_ref.shape[1] - 256 :])


def join_kernel(keep_ref, rows_ref, cols_ref, out_ref):
    sequences, _, features = out_ref.shape
    total = keep_ref[...] + rows_ref[:, 0 : keep_ref.shape[1]].astype(F32) + cols_ref[...].astype(F32)
    for s in range(sequences):
        out_ref[s] = total[:, s * features : (s + 1) * features]


def body(
    layernormed_alignment,
    average_cotangent,
    sequence_validity,
    residue_validity,
    pair_scores,
    payload_projection,
    sigmoid_projection,
    final_projection,
):
    row_count = lax.axis_size("row")
    col_count = lax.axis_size("col")
    seq_count = lax.axis_size("seq")
    row_pos = lax.axis_index("row")
    col_pos = lax.axis_index("col")
    seq_pos = lax.axis_index("seq")
    sequences, rows, features = layernormed_alignment.shape
    heads, _, columns = pair_scores.shape
    width = payload_projection.shape[1]
    dim = width // heads
    stretch = rows // col_count
    wide = sequences * features
    own = heads // seq_count
    group = sequences // STEPS
    side = row_count // 2
    core, plane, across = row_pos % 2, col_pos % 2, col_pos // 2
    place = jnp.stack([core, plane, across, seq_pos]).astype(jnp.int32)

    tokens = far(jnp.swapaxes(layernormed_alignment, 1, 2))
    cotangent = far(jnp.swapaxes(average_cotangent, 1, 2))
    scores = far(pair_scores)
    payload_w = far(payload_projection)
    gate_w = far(sigmoid_projection)
    final_w = far(final_projection.T)
    keep = lax.dynamic_slice_in_dim(residue_validity, col_pos * columns, columns, 0).reshape(1, columns)

    at = lambda x, core, y, z: (x * 2 + core) * col_count + y * 2 + z
    routes = [
        (at(a, z, b, z), at((b + 2 * a) % side, 1 - z, a, z))
        for a in range(side)
        for b in range(side)
        for z in range(2)
    ]
    mine = lax.ppermute(jnp.swapaxes(layernormed_alignment, 1, 2), ("row", "col"), routes)

    local_stats = call(
        stats_kernel,
        jax.ShapeDtypeStruct((col_count, 2 * heads, rows), F32),
        [scores, keep],
        moved=4 << 20,
    )
    stats = lax.all_to_all(local_stats, "col", 0, 0, tiled=True)

    mine, stats = lax.optimization_barrier((mine, stats))
    other = lax.ppermute(mine, "row", [(i, i ^ 1) for i in range(row_count)])

    message = wide + 256
    pieces = pltpu.VMEM((group, width, rows), BF16)
    square = pltpu.VMEM((heads, rows, columns), F32)
    weights, col_term, *sent = call(
        main_kernel,
        [jax.ShapeDtypeStruct((own, rows, columns), F32), jax.ShapeDtypeStruct((row_count, stretch, wide), BF16)]
        + [jax.ShapeDtypeStruct((2, stretch, message), BF16)]
        + [pltpu.HBM((2, stretch, message), BF16)] * (side - 1)
        + [jax.ShapeDtypeStruct((own + 1, rows, 128), BF16)] * seq_count,
        [scores, keep, stats, tokens, cotangent, far(sequence_validity), mine, other, payload_w, gate_w, final_w],
        [
            whole((heads, rows, columns)),
            whole((1, columns)),
            whole((col_count, 2 * heads, rows)),
            by_step(group, features, rows),
            by_step(group, features, rows),
            by_step(group, rows),
            whole((sequences, features, rows)),
            whole((sequences, features, rows)),
            whole((features, width)),
            whole((features, width)),
            whole((features, width)),
        ],
        [whole((own, rows, columns)), whole((row_count, stretch, wide))]
        + [whole((2, stretch, message)) for _ in range(side)]
        + [whole((own + 1, rows, 128)) for _ in range(seq_count)],
        grid=(STEPS,),
        scratch=[
            pltpu.VMEM((3, width, features), BF16),
            square,
            pltpu.VMEM((heads, rows, columns), BF16),
            pltpu.VMEM((heads, columns, rows), BF16),
            pieces,
            pltpu.VMEM((group, width, rows), F32),
            pieces,
            pieces,
            pltpu.VMEM((col_count, stretch, wide), BF16),
            square,
            pltpu.VMEM((seq_count, own + 1, rows, 128), BF16),
        ],
        scalars=place,
        flops=1 << 30,
        moved=18 << 20,
    )
    row_term, d_weights = sent[:side], sent[side:]

    def swapped(a, axis, bits):
        return lax.ppermute(a, axis, [(i, i ^ bits) for i in range(lax.axis_size(axis))])

    row_term = row_term[:1] + [swapped(row_term[k], "col", 2 * k) for k in range(1, side)]
    d_weights = d_weights[:1] + [swapped(d_weights[k], "seq", k) for k in range(1, seq_count)]
    col_term = lax.all_to_all(col_term, "row", 0, 0, tiled=True)
    col_term = jnp.sum(col_term.astype(F32), axis=0).astype(BF16)
    col_term = lax.ppermute(
        col_term,
        ("row", "col"),
        [(r * col_count + c, c * col_count + r) for r in range(row_count) for c in range(col_count)],
    )
    row_keep, inner, row_send = call(
        fold_kernel,
        [
            jax.ShapeDtypeStruct((stretch, wide), F32),
            jax.ShapeDtypeStruct((heads, 256), F32),
            jax.ShapeDtypeStruct((stretch, message), BF16),
        ],
        row_term,
        scalars=place,
        moved=2 << 20,
    )
    row_send = swapped(row_send, "col", 1)
    inner = call(inner_kernel, jax.ShapeDtypeStruct((heads, 256), F32), [inner, row_send], moved=1 << 20)
    inners = [inner] + [swapped(inner, "seq", k) for k in range(1, seq_count)]
    score_cotangent = call(
        score_kernel,
        jax.ShapeDtypeStruct((own, rows, columns), F32),
        d_weights + inners + [weights],
        scalars=place,
        moved=2 << 20,
    )
    alignment_cotangent = call(
        join_kernel,
        jax.ShapeDtypeStruct((sequences, stretch, features), F32),
        [row_keep, row_send, col_term],
        moved=2 << 20,
    )
    return (alignment_cotangent, score_cotangent)


def solution(mesh):
    return jax.shard_map(
        body,
        mesh=mesh,
        in_specs=(
            P("seq", "row", None),
            P("seq", "row", None),
            P("seq", "row"),
            P(),
            P(None, "row", "col"),
            P(),
            P(),
            P(),
        ),
        out_specs=(P("seq", ("row", "col"), None), P("seq", "row", "col")),
        check_vma=False,
    )
```

```python
import jax
import jax.numpy as jnp
from jax import lax
from jax.experimental import pallas as pl
from jax.experimental.pallas import tpu as pltpu
from jax.sharding import PartitionSpec as P

F32 = jnp.float32
BF16 = jnp.bfloat16
MASKED = -1000000000.0
VMEM_BYTES = 32 * 1024 * 1024
STEPS = 2


def call(kernel, outs, inputs, in_specs=None, out_specs=None, grid=None, scratch=(), scalars=None, flops=0, moved=0):
    local = lambda: pl.BlockSpec(memory_space=pltpu.VMEM)
    several = isinstance(outs, list)
    operands = [] if scalars is None else [scalars]
    if in_specs is None:
        in_specs = [local() for _ in inputs]
    if out_specs is None:
        out_specs = [local() for _ in outs] if several else local()
    extra = {} if grid is None else {"grid": grid}
    return pl.pallas_call(
        kernel,
        out_shape=outs,
        in_specs=[pl.BlockSpec(memory_space=pltpu.SMEM)] * len(operands) + in_specs,
        out_specs=out_specs,
        scratch_shapes=list(scratch),
        compiler_params=pltpu.CompilerParams(vmem_limit_bytes=VMEM_BYTES),
        cost_estimate=pl.CostEstimate(flops=flops, bytes_accessed=moved, transcendentals=0),
        **extra,
    )(*operands, *inputs)


def whole(shape):
    return pl.BlockSpec(shape, lambda i: (0,) * len(shape))


def by_step(*dims):
    return pl.BlockSpec(dims, lambda i: (i,) + (0,) * (len(dims) - 1))


def far(a):
    return pltpu.with_memory_space_constraint(a, pltpu.HBM)


def dot(a, b):
    return jnp.dot(a, b, preferred_element_type=F32)


def dot_last(a, b):
    return lax.dot_general(a, b, (((1,), (1,)), ((), ())), preferred_element_type=F32)


def turned(a):
    return a.astype(F32).T.astype(a.dtype)


def stats_kernel(scores_ref, keep_ref, stats_ref):
    heads, rows, _ = scores_ref.shape
    keep = keep_ref[...] > 0
    lane = lax.broadcasted_iota(jnp.int32, (rows, 128), 1)
    table = jnp.zeros((rows, 128), F32)
    for h in range(heads):
        masked = jnp.where(keep, scores_ref[h], MASKED)
        peak = jnp.max(masked, axis=1, keepdims=True)
        total = jnp.sum(jnp.exp(masked - peak), axis=1, keepdims=True)
        table = jnp.where(lane == h, peak, table)
        table = jnp.where(lane == heads + h, total, table)
    packed = table.T[0 : 2 * heads]
    for k in range(stats_ref.shape[0]):
        stats_ref[k] = packed


def project_rows(weight, pieces, out_ref, first):
    sequences = pieces.shape[0]
    chunks, stretch, _ = out_ref.shape
    features = weight.shape[0]
    for s in range(0, sequences, 2):
        pair = [dot(weight, pieces[s + k]) for k in (0, 1)]
        rows = jnp.concatenate(pair, axis=0).T.reshape(chunks, stretch, 2 * features)
        lanes = pl.ds(pl.multiple_of((first + s) * features, 128), 2 * features)
        out_ref[:, :, lanes] = rows.astype(out_ref.dtype)


def thirds(table):
    first = table.astype(BF16)
    rest = table - first.astype(F32)
    second = rest.astype(BF16)
    third = (rest - second.astype(F32)).astype(BF16)
    return jnp.concatenate([t.astype(F32) for t in (first, second, third)], axis=0).astype(BF16)


def joined(table):
    count = table.shape[0] // 3
    table = table.astype(F32)
    return table[0:count] + table[count : 2 * count] + table[2 * count : 3 * count]


def main_kernel(
    place_ref,
    scores_ref,
    keep_ref,
    stats_ref,
    x_ref,
    cot_ref,
    mask_ref,
    mine_ref,
    other_ref,
    payload_ref,
    gate_w_ref,
    final_w_ref,
    weights_ref,
    col_ref,
    row0_ref,
    row1_ref,
    row2_ref,
    row3_ref,
    pair0_ref,
    pair1_ref,
    pair2_ref,
    pair3_ref,
    wt,
    weights,
    wb,
    att,
    term,
    values,
    pieces,
    row_out,
    pair_sum,
    pair_out,
):
    step = pl.program_id(0)
    heads, rows, columns = scores_ref.shape
    group = x_ref.shape[0]
    width = payload_ref.shape[1]
    dim = width // heads
    wide = col_ref.shape[2]

    @pl.when(step == 0)
    def _():
        for k, weight in enumerate((payload_ref, gate_w_ref, final_w_ref)):
            wt[k] = turned(weight[...])
        pair_sum[...] = jnp.zeros(pair_sum.shape, F32)
        peaks = stats_ref[:, 0:heads]
        peak = jnp.max(peaks, axis=0)
        total = jnp.sum(stats_ref[:, heads : 2 * heads] * jnp.exp(peaks - peak[None]), axis=0)
        table = jnp.concatenate([peak, 1.0 / total, jnp.zeros((128 - 2 * heads, rows), F32)], axis=0).T
        keep = keep_ref[...] > 0
        for h in range(heads):
            masked = jnp.where(keep, scores_ref[h], MASKED)
            exact = jnp.exp(masked - table[:, h : h + 1]) * table[:, heads + h : heads + h + 1]
            weights[h] = exact
            wb[h] = exact.astype(BF16)

    first = pl.multiple_of(step * group, group)
    mask = mask_ref[...].astype(F32)
    for k in range(group):
        gate = 1.0 / (1.0 + jnp.exp(-dot(wt[1], x_ref[k])))
        cot = dot(wt[2], cot_ref[k]) * mask[k : k + 1]
        exact = cot * gate
        att[k] = exact.astype(BF16)
        term[k] = exact * (1.0 - gate)
    for h in range(heads):
        block = att[:, h * dim : (h + 1) * dim, :].reshape(group * dim, rows)
        pieces[:, h * dim : (h + 1) * dim, :] = dot(block, wb[h]).astype(BF16).reshape(group, dim, columns)
    project_rows(payload_ref[...], pieces, col_ref, first)

    own = place_ref[0] != place_ref[1]
    tokens = jnp.where(own, mine_ref[pl.ds(first, group)], other_ref[pl.ds(first, group)])
    for k in range(group):
        values[k] = dot(wt[0], tokens[k]).astype(BF16)
    for h in range(heads):
        block = values[:, h * dim : (h + 1) * dim, :].reshape(group * dim, columns)
        average = dot_last(block, wb[h]).reshape(group, dim, rows)
        pieces[:, h * dim : (h + 1) * dim, :] = (average * term[:, h * dim : (h + 1) * dim, :]).astype(BF16)
        att_rows = turned(att[:, h * dim : (h + 1) * dim, :].reshape(group * dim, rows))
        pair_sum[h] += dot(att_rows, block)
    project_rows(gate_w_ref[...], pieces, row_out, first)

    @pl.when(step == pl.num_programs(0) - 1)
    def _():
        lane = lax.broadcasted_iota(jnp.int32, (rows, 128), 1)
        table = jnp.zeros((rows, 128), F32)
        owners = pair_out.shape[0]
        own_heads = heads // owners
        for k in range(owners):
            tails = []
            for g in range(own_heads):
                h = k * own_heads + g
                grad = pair_sum[h].astype(BF16)
                pair_out[k, g] = grad[:, 0:128]
                tails.append(grad[:, 128:192])
                inner = jnp.sum(weights[h] * grad.astype(F32), axis=1, keepdims=True)
                table = jnp.where(lane == h, inner, table)
            pair_out[k, own_heads] = jnp.concatenate(tails, axis=-1)
        inner = thirds(jnp.concatenate([table.T[0:heads], jnp.zeros((heads, 256 - rows), F32)], axis=-1))
        for k, out_ref in enumerate((row0_ref, row1_ref, row2_ref, row3_ref)):
            out_ref[:, :, 0:wide] = row_out[pl.ds(2 * (place_ref[2] ^ k), 2)]
            for z in range(2):
                out_ref[z, :, wide:] = inner[:, 128 * z : 128 * z + 128]
        for k, out_ref in enumerate((pair0_ref, pair1_ref, pair2_ref, pair3_ref)):
            out_ref[...] = pair_out[place_ref[3] ^ k]
        weights_ref[...] = weights[pl.ds(place_ref[3] * own_heads, own_heads)]


def score_kernel(
    place_ref,
    part0_ref,
    part1_ref,
    part2_ref,
    part3_ref,
    inner0_ref,
    inner1_ref,
    inner2_ref,
    inner3_ref,
    weights_ref,
    out_ref,
):
    heads, rows, _ = out_ref.shape
    total = part0_ref[...].astype(F32)
    for part in (part1_ref, part2_ref, part3_ref):
        total = total + part[...].astype(F32)
    inner = ((inner0_ref[...] + inner1_ref[...]) + (inner2_ref[...] + inner3_ref[...]))[:, 0:rows]
    table = jnp.concatenate([inner, jnp.zeros((128 - inner.shape[0], rows), F32)], axis=0).T
    lane = lax.broadcasted_iota(jnp.int32, table.shape, 1)
    for h in range(heads):
        mine = place_ref[3] * heads + h
        grad = jnp.concatenate([total[h], total[heads][:, 64 * h : 64 * h + 64]], axis=-1)
        own = jnp.sum(jnp.where(lane == mine, table, 0.0), axis=1, keepdims=True)
        out_ref[h] = weights_ref[h] * (grad - own)


def total_kernel(parts_ref, out_ref):
    out_ref[...] = jnp.sum(parts_ref[...].astype(F32), axis=0).astype(BF16)


def fold_kernel(place_ref, part0_ref, part1_ref, part2_ref, part3_ref, keep_ref, inner_ref, send_ref):
    wide = keep_ref.shape[1]
    parts = (part0_ref, part1_ref, part2_ref, part3_ref)
    total = sum(part[:, :, 0:wide].astype(F32) for part in parts)
    high = place_ref[1] == 1
    keep_ref[...] = jnp.where(high, total[1], total[0])
    send_ref[:, 0:wide] = jnp.where(high, total[0], total[1]).astype(BF16)
    inner = sum(joined(jnp.concatenate([part[0, :, wide:], part[1, :, wide:]], axis=-1)) for part in parts)
    inner_ref[...] = inner
    send_ref[:, wide:] = thirds(inner)


def inner_kernel(inner_ref, rows_ref, out_ref):
    out_ref[...] = inner_ref[...] + joined(rows_ref[:, rows_ref.shape[1] - 256 :])


def join_kernel(keep_ref, rows_ref, cols_ref, out_ref):
    sequences, _, features = out_ref.shape
    total = keep_ref[...] + rows_ref[:, 0 : keep_ref.shape[1]].astype(F32) + cols_ref[...].astype(F32)
    for s in range(sequences):
        out_ref[s] = total[:, s * features : (s + 1) * features]


def body(
    layernormed_alignment,
    average_cotangent,
    sequence_validity,
    residue_validity,
    pair_scores,
    payload_projection,
    sigmoid_projection,
    final_projection,
):
    row_count = lax.axis_size("row")
    col_count = lax.axis_size("col")
    seq_count = lax.axis_size("seq")
    row_pos = lax.axis_index("row")
    col_pos = lax.axis_index("col")
    seq_pos = lax.axis_index("seq")
    sequences, rows, features = layernormed_alignment.shape
    heads, _, columns = pair_scores.shape
    width = payload_projection.shape[1]
    dim = width // heads
    stretch = rows // col_count
    wide = sequences * features
    own = heads // seq_count
    group = sequences // STEPS
    side = row_count // 2
    core, plane, across = row_pos % 2, col_pos % 2, col_pos // 2
    place = jnp.stack([core, plane, across, seq_pos]).astype(jnp.int32)

    tokens = far(jnp.swapaxes(layernormed_alignment, 1, 2))
    cotangent = far(jnp.swapaxes(average_cotangent, 1, 2))
    scores = far(pair_scores)
    payload_w = far(payload_projection)
    gate_w = far(sigmoid_projection)
    final_w = far(final_projection.T)
    keep = lax.dynamic_slice_in_dim(residue_validity, col_pos * columns, columns, 0).reshape(1, columns)

    at = lambda x, core, y, z: (x * 2 + core) * col_count + y * 2 + z
    routes = [
        (at(a, z, b, z), at((b + 2 * a) % side, 1 - z, a, z))
        for a in range(side)
        for b in range(side)
        for z in range(2)
    ]
    mine = lax.ppermute(jnp.swapaxes(layernormed_alignment, 1, 2), ("row", "col"), routes)

    local_stats = call(
        stats_kernel,
        jax.ShapeDtypeStruct((col_count, 2 * heads, rows), F32),
        [scores, keep],
        moved=4 << 20,
    )
    stats = lax.all_to_all(local_stats, "col", 0, 0, tiled=True)

    mine, stats = lax.optimization_barrier((mine, stats))
    other = lax.ppermute(mine, "row", [(i, i ^ 1) for i in range(row_count)])

    message = wide + 256
    half_message = wide + 128
    pieces = pltpu.VMEM((group, width, rows), BF16)
    square = pltpu.VMEM((heads, rows, columns), F32)
    weights, col_term, *sent = call(
        main_kernel,
        [jax.ShapeDtypeStruct((own, rows, columns), F32), jax.ShapeDtypeStruct((row_count, stretch, wide), BF16)]
        + [jax.ShapeDtypeStruct((2, stretch, half_message), BF16)]
        + [pltpu.HBM((2, stretch, half_message), BF16)] * (side - 1)
        + [jax.ShapeDtypeStruct((own + 1, rows, 128), BF16)] * seq_count,
        [scores, keep, stats, tokens, cotangent, far(sequence_validity), mine, other, payload_w, gate_w, final_w],
        [
            whole((heads, rows, columns)),
            whole((1, columns)),
            whole((col_count, 2 * heads, rows)),
            by_step(group, features, rows),
            by_step(group, features, rows),
            by_step(group, rows),
            whole((sequences, features, rows)),
            whole((sequences, features, rows)),
            whole((features, width)),
            whole((features, width)),
            whole((features, width)),
        ],
        [whole((own, rows, columns)), whole((row_count, stretch, wide))]
        + [whole((2, stretch, half_message)) for _ in range(side)]
        + [whole((own + 1, rows, 128)) for _ in range(seq_count)],
        grid=(STEPS,),
        scratch=[
            pltpu.VMEM((3, width, features), BF16),
            square,
            pltpu.VMEM((heads, rows, columns), BF16),
            pieces,
            pltpu.VMEM((group, width, rows), F32),
            pieces,
            pieces,
            pltpu.VMEM((col_count, stretch, wide), BF16),
            square,
            pltpu.VMEM((seq_count, own + 1, rows, 128), BF16),
        ],
        scalars=place,
        flops=1 << 30,
        moved=18 << 20,
    )
    row_term, d_weights = sent[:side], sent[side:]

    def swapped(a, axis, bits):
        return lax.ppermute(a, axis, [(i, i ^ bits) for i in range(lax.axis_size(axis))])

    row_term = row_term[:1] + [swapped(row_term[k], "col", 2 * k) for k in range(1, side)]
    d_weights = d_weights[:1] + [swapped(d_weights[k], "seq", k) for k in range(1, seq_count)]
    col_term = lax.all_to_all(col_term, "row", 0, 0, tiled=True)
    col_term = call(total_kernel, jax.ShapeDtypeStruct((stretch, wide), BF16), [col_term], moved=1 << 20)
    col_term, row_term[3] = lax.optimization_barrier((col_term, row_term[3]))
    col_term = lax.ppermute(
        col_term,
        ("row", "col"),
        [(r * col_count + c, c * col_count + r) for r in range(row_count) for c in range(col_count)],
    )
    row_keep, inner, row_send = call(
        fold_kernel,
        [
            jax.ShapeDtypeStruct((stretch, wide), F32),
            jax.ShapeDtypeStruct((heads, 256), F32),
            jax.ShapeDtypeStruct((stretch, message), BF16),
        ],
        row_term,
        scalars=place,
        moved=2 << 20,
    )
    row_send = swapped(row_send, "col", 1)
    inner = call(inner_kernel, jax.ShapeDtypeStruct((heads, 256), F32), [inner, row_send], moved=1 << 20)
    inners = [inner] + [swapped(inner, "seq", k) for k in range(1, seq_count)]
    score_cotangent = call(
        score_kernel,
        jax.ShapeDtypeStruct((own, rows, columns), F32),
        d_weights + inners + [weights],
        scalars=place,
        moved=2 << 20,
    )
    alignment_cotangent = call(
        join_kernel,
        jax.ShapeDtypeStruct((sequences, stretch, features), F32),
        [row_keep, row_send, col_term],
        moved=2 << 20,
    )
    return (alignment_cotangent, score_cotangent)


def solution(mesh):
    return jax.shard_map(
        body,
        mesh=mesh,
        in_specs=(
            P("seq", "row", None),
            P("seq", "row", None),
            P("seq", "row"),
            P(),
            P(None, "row", "col"),
            P(),
            P(),
            P(),
        ),
        out_specs=(P("seq", ("row", "col"), None), P("seq", "row", "col")),
        check_vma=False,
    )
```

```python
import jax
import jax.numpy as jnp
from jax import lax
from jax.experimental import pallas as pl
from jax.experimental.pallas import tpu as pltpu
from jax.sharding import PartitionSpec as P

F32 = jnp.float32
BF16 = jnp.bfloat16
MASKED = -1000000000.0
VMEM_BYTES = 32 * 1024 * 1024
STEPS = 2


def call(kernel, outs, inputs, in_specs=None, out_specs=None, grid=None, scratch=(), scalars=None, flops=0, moved=0):
    local = lambda: pl.BlockSpec(memory_space=pltpu.VMEM)
    several = isinstance(outs, list)
    operands = [] if scalars is None else [scalars]
    if in_specs is None:
        in_specs = [local() for _ in inputs]
    if out_specs is None:
        out_specs = [local() for _ in outs] if several else local()
    extra = {} if grid is None else {"grid": grid}
    return pl.pallas_call(
        kernel,
        out_shape=outs,
        in_specs=[pl.BlockSpec(memory_space=pltpu.SMEM)] * len(operands) + in_specs,
        out_specs=out_specs,
        scratch_shapes=list(scratch),
        compiler_params=pltpu.CompilerParams(vmem_limit_bytes=VMEM_BYTES),
        cost_estimate=pl.CostEstimate(flops=flops, bytes_accessed=moved, transcendentals=0),
        **extra,
    )(*operands, *inputs)


def whole(shape):
    return pl.BlockSpec(shape, lambda i: (0,) * len(shape))


def by_step(*dims):
    return pl.BlockSpec(dims, lambda i: (i,) + (0,) * (len(dims) - 1))


def far(a):
    return pltpu.with_memory_space_constraint(a, pltpu.HBM)


def dot(a, b):
    return jnp.dot(a, b, preferred_element_type=F32)


def dot_last(a, b):
    return lax.dot_general(a, b, (((1,), (1,)), ((), ())), preferred_element_type=F32)


def turned(a):
    return a.astype(F32).T.astype(a.dtype)


def stats_kernel(scores_ref, keep_ref, stats_ref):
    heads, rows, _ = scores_ref.shape
    keep = keep_ref[...] > 0
    lane = lax.broadcasted_iota(jnp.int32, (rows, 128), 1)
    table = jnp.zeros((rows, 128), F32)
    for h in range(heads):
        masked = jnp.where(keep, scores_ref[h], MASKED)
        peak = jnp.max(masked, axis=1, keepdims=True)
        total = jnp.sum(jnp.exp(masked - peak), axis=1, keepdims=True)
        table = jnp.where(lane == h, peak, table)
        table = jnp.where(lane == heads + h, total, table)
    packed = table.T[0 : 2 * heads]
    for k in range(stats_ref.shape[0]):
        stats_ref[k] = packed


def project_rows(weight, pieces, out_ref, first):
    sequences = pieces.shape[0]
    chunks, stretch, _ = out_ref.shape
    features = weight.shape[0]
    for s in range(0, sequences, 2):
        pair = [dot(weight, pieces[s + k]) for k in (0, 1)]
        rows = jnp.concatenate(pair, axis=0).T.reshape(chunks, stretch, 2 * features)
        lanes = pl.ds(pl.multiple_of((first + s) * features, 128), 2 * features)
        out_ref[:, :, lanes] = rows.astype(out_ref.dtype)


def thirds(table):
    first = table.astype(BF16)
    rest = table - first.astype(F32)
    second = rest.astype(BF16)
    third = (rest - second.astype(F32)).astype(BF16)
    return jnp.concatenate([t.astype(F32) for t in (first, second, third)], axis=0).astype(BF16)


def joined(table):
    count = table.shape[0] // 3
    table = table.astype(F32)
    return table[0:count] + table[count : 2 * count] + table[2 * count : 3 * count]


def main_kernel(
    place_ref,
    scores_ref,
    keep_ref,
    stats_ref,
    x_ref,
    cot_ref,
    mask_ref,
    mine_ref,
    other_ref,
    payload_ref,
    gate_w_ref,
    final_w_ref,
    weights_ref,
    col_ref,
    row0_ref,
    row1_ref,
    row2_ref,
    row3_ref,
    pair0_ref,
    pair1_ref,
    pair2_ref,
    pair3_ref,
    wt,
    weights,
    wb,
    att,
    term,
    values,
    pieces,
    row_out,
    pair_sum,
    pair_out,
):
    step = pl.program_id(0)
    heads, rows, columns = scores_ref.shape
    group = x_ref.shape[0]
    width = payload_ref.shape[1]
    dim = width // heads
    wide = col_ref.shape[2]

    @pl.when(step == 0)
    def _():
        for k, weight in enumerate((payload_ref, gate_w_ref, final_w_ref)):
            wt[k] = turned(weight[...])
        pair_sum[...] = jnp.zeros(pair_sum.shape, F32)
        peaks = stats_ref[:, 0:heads]
        peak = jnp.max(peaks, axis=0)
        total = jnp.sum(stats_ref[:, heads : 2 * heads] * jnp.exp(peaks - peak[None]), axis=0)
        table = jnp.concatenate([peak, 1.0 / total, jnp.zeros((128 - 2 * heads, rows), F32)], axis=0).T
        keep = keep_ref[...] > 0
        for h in range(heads):
            masked = jnp.where(keep, scores_ref[h], MASKED)
            exact = jnp.exp(masked - table[:, h : h + 1]) * table[:, heads + h : heads + h + 1]
            weights[h] = exact
            wb[h] = exact.astype(BF16)

    first = pl.multiple_of(step * group, group)
    mask = mask_ref[...].astype(F32)
    for k in range(group):
        gate = 1.0 / (1.0 + jnp.exp(-dot(wt[1], x_ref[k])))
        cot = dot(wt[2], cot_ref[k]) * mask[k : k + 1]
        exact = cot * gate
        att[k] = exact.astype(BF16)
        term[k] = exact * (1.0 - gate)
    for h in range(heads):
        block = att[:, h * dim : (h + 1) * dim, :].reshape(group * dim, rows)
        pieces[:, h * dim : (h + 1) * dim, :] = dot(block, wb[h]).astype(BF16).reshape(group, dim, columns)
    project_rows(payload_ref[...], pieces, col_ref, first)

    own = place_ref[0] != place_ref[1]
    tokens = jnp.where(own, mine_ref[pl.ds(first, group)], other_ref[pl.ds(first, group)])
    for k in range(group):
        values[k] = dot(wt[0], tokens[k]).astype(BF16)
    for h in range(heads):
        block = values[:, h * dim : (h + 1) * dim, :].reshape(group * dim, columns)
        average = dot_last(block, wb[h]).reshape(group, dim, rows)
        pieces[:, h * dim : (h + 1) * dim, :] = (average * term[:, h * dim : (h + 1) * dim, :]).astype(BF16)
        att_rows = turned(att[:, h * dim : (h + 1) * dim, :].reshape(group * dim, rows))
        pair_sum[h] += dot(att_rows, block)
    project_rows(gate_w_ref[...], pieces, row_out, first)

    @pl.when(step == pl.num_programs(0) - 1)
    def _():
        lane = lax.broadcasted_iota(jnp.int32, (rows, 128), 1)
        table = jnp.zeros((rows, 128), F32)
        owners = pair_out.shape[0]
        own_heads = heads // owners
        for k in range(owners):
            tails = []
            for g in range(own_heads):
                h = k * own_heads + g
                grad = pair_sum[h].astype(BF16)
                pair_out[k, g] = grad[:, 0:128]
                tails.append(grad[:, 128:192])
                inner = jnp.sum(weights[h] * grad.astype(F32), axis=1, keepdims=True)
                table = jnp.where(lane == h, inner, table)
            pair_out[k, own_heads] = jnp.concatenate(tails, axis=-1)
        inner = thirds(jnp.concatenate([table.T[0:heads], jnp.zeros((heads, 256 - rows), F32)], axis=-1))
        for k, out_ref in enumerate((row0_ref, row1_ref, row2_ref, row3_ref)):
            out_ref[:, :, 0:wide] = row_out[pl.ds(2 * (place_ref[2] ^ k), 2)]
            for z in range(2):
                out_ref[z, :, wide:] = inner[:, 128 * z : 128 * z + 128]
        for k, out_ref in enumerate((pair0_ref, pair1_ref, pair2_ref, pair3_ref)):
            out_ref[...] = pair_out[place_ref[3] ^ k]
        weights_ref[...] = weights[pl.ds(place_ref[3] * own_heads, own_heads)]


def gradient_kernel(part0_ref, part1_ref, part2_ref, part3_ref, out_ref):
    heads = out_ref.shape[0]
    total = part0_ref[...].astype(F32)
    for part in (part1_ref, part2_ref, part3_ref):
        total = total + part[...].astype(F32)
    for h in range(heads):
        grad = jnp.concatenate([total[h], total[heads][:, 64 * h : 64 * h + 64]], axis=-1)
        out_ref[h] = grad


def score_kernel(place_ref, inner0_ref, inner1_ref, inner2_ref, inner3_ref, grad_ref, weights_ref, out_ref):
    heads, rows, _ = out_ref.shape
    inner = ((inner0_ref[...] + inner1_ref[...]) + (inner2_ref[...] + inner3_ref[...]))[:, 0:rows]
    table = jnp.concatenate([inner, jnp.zeros((128 - inner.shape[0], rows), F32)], axis=0).T
    lane = lax.broadcasted_iota(jnp.int32, table.shape, 1)
    for h in range(heads):
        mine = place_ref[3] * heads + h
        own = jnp.sum(jnp.where(lane == mine, table, 0.0), axis=1, keepdims=True)
        out_ref[h] = weights_ref[h] * (grad_ref[h] - own)


def total_kernel(parts_ref, out_ref):
    out_ref[...] = jnp.sum(parts_ref[...].astype(F32), axis=0).astype(BF16)


def fold_kernel(place_ref, part0_ref, part1_ref, part2_ref, part3_ref, keep_ref, inner_ref, send_ref):
    wide = keep_ref.shape[1]
    parts = (part0_ref, part1_ref, part2_ref, part3_ref)
    total = sum(part[:, :, 0:wide].astype(F32) for part in parts)
    high = place_ref[1] == 1
    keep_ref[...] = jnp.where(high, total[1], total[0])
    send_ref[:, 0:wide] = jnp.where(high, total[0], total[1]).astype(BF16)
    inner = sum(joined(jnp.concatenate([part[0, :, wide:], part[1, :, wide:]], axis=-1)) for part in parts)
    inner_ref[...] = inner
    send_ref[:, wide:] = thirds(inner)


def inner_kernel(inner_ref, rows_ref, out_ref):
    out_ref[...] = inner_ref[...] + joined(rows_ref[:, rows_ref.shape[1] - 256 :])


def join_kernel(keep_ref, rows_ref, cols_ref, out_ref):
    sequences, _, features = out_ref.shape
    total = keep_ref[...] + rows_ref[:, 0 : keep_ref.shape[1]].astype(F32) + cols_ref[...].astype(F32)
    for s in range(sequences):
        out_ref[s] = total[:, s * features : (s + 1) * features]


def body(
    layernormed_alignment,
    average_cotangent,
    sequence_validity,
    residue_validity,
    pair_scores,
    payload_projection,
    sigmoid_projection,
    final_projection,
):
    row_count = lax.axis_size("row")
    col_count = lax.axis_size("col")
    seq_count = lax.axis_size("seq")
    row_pos = lax.axis_index("row")
    col_pos = lax.axis_index("col")
    seq_pos = lax.axis_index("seq")
    sequences, rows, features = layernormed_alignment.shape
    heads, _, columns = pair_scores.shape
    width = payload_projection.shape[1]
    dim = width // heads
    stretch = rows // col_count
    wide = sequences * features
    own = heads // seq_count
    group = sequences // STEPS
    side = row_count // 2
    core, plane, across = row_pos % 2, col_pos % 2, col_pos // 2
    place = jnp.stack([core, plane, across, seq_pos]).astype(jnp.int32)

    tokens = far(jnp.swapaxes(layernormed_alignment, 1, 2))
    cotangent = far(jnp.swapaxes(average_cotangent, 1, 2))
    scores = far(pair_scores)
    payload_w = far(payload_projection)
    gate_w = far(sigmoid_projection)
    final_w = far(final_projection.T)
    keep = lax.dynamic_slice_in_dim(residue_validity, col_pos * columns, columns, 0).reshape(1, columns)

    at = lambda x, core, y, z: (x * 2 + core) * col_count + y * 2 + z
    routes = [
        (at(a, z, b, z), at((b + 2 * a) % side, 1 - z, a, z))
        for a in range(side)
        for b in range(side)
        for z in range(2)
    ]
    mine = lax.ppermute(jnp.swapaxes(layernormed_alignment, 1, 2), ("row", "col"), routes)

    local_stats = call(
        stats_kernel,
        jax.ShapeDtypeStruct((col_count, 2 * heads, rows), F32),
        [scores, keep],
        moved=4 << 20,
    )
    stats = lax.all_to_all(local_stats, "col", 0, 0, tiled=True)

    mine, stats = lax.optimization_barrier((mine, stats))
    other = lax.ppermute(mine, "row", [(i, i ^ 1) for i in range(row_count)])

    message = wide + 256
    half_message = wide + 128
    pieces = pltpu.VMEM((group, width, rows), BF16)
    square = pltpu.VMEM((heads, rows, columns), F32)
    weights, col_term, *sent = call(
        main_kernel,
        [jax.ShapeDtypeStruct((own, rows, columns), F32), jax.ShapeDtypeStruct((row_count, stretch, wide), BF16)]
        + [jax.ShapeDtypeStruct((2, stretch, half_message), BF16)]
        + [pltpu.HBM((2, stretch, half_message), BF16)] * (side - 1)
        + [jax.ShapeDtypeStruct((own + 1, rows, 128), BF16)] * seq_count,
        [scores, keep, stats, tokens, cotangent, far(sequence_validity), mine, other, payload_w, gate_w, final_w],
        [
            whole((heads, rows, columns)),
            whole((1, columns)),
            whole((col_count, 2 * heads, rows)),
            by_step(group, features, rows),
            by_step(group, features, rows),
            by_step(group, rows),
            whole((sequences, features, rows)),
            whole((sequences, features, rows)),
            whole((features, width)),
            whole((features, width)),
            whole((features, width)),
        ],
        [whole((own, rows, columns)), whole((row_count, stretch, wide))]
        + [whole((2, stretch, half_message)) for _ in range(side)]
        + [whole((own + 1, rows, 128)) for _ in range(seq_count)],
        grid=(STEPS,),
        scratch=[
            pltpu.VMEM((3, width, features), BF16),
            square,
            pltpu.VMEM((heads, rows, columns), BF16),
            pieces,
            pltpu.VMEM((group, width, rows), F32),
            pieces,
            pieces,
            pltpu.VMEM((col_count, stretch, wide), BF16),
            square,
            pltpu.VMEM((seq_count, own + 1, rows, 128), BF16),
        ],
        scalars=place,
        flops=1 << 30,
        moved=18 << 20,
    )
    row_term, d_weights = sent[:side], sent[side:]

    def swapped(a, axis, bits):
        return lax.ppermute(a, axis, [(i, i ^ bits) for i in range(lax.axis_size(axis))])

    row_term = row_term[:1] + [swapped(row_term[k], "col", 2 * k) for k in range(1, side)]
    d_weights = d_weights[:1] + [swapped(d_weights[k], "seq", k) for k in range(1, seq_count)]
    col_term = lax.all_to_all(col_term, "row", 0, 0, tiled=True)
    col_term = call(total_kernel, jax.ShapeDtypeStruct((stretch, wide), BF16), [col_term], moved=1 << 20)
    col_term, row_term[3] = lax.optimization_barrier((col_term, row_term[3]))
    col_term = lax.ppermute(
        col_term,
        ("row", "col"),
        [(r * col_count + c, c * col_count + r) for r in range(row_count) for c in range(col_count)],
    )
    row_keep, inner, row_send = call(
        fold_kernel,
        [
            jax.ShapeDtypeStruct((stretch, wide), F32),
            jax.ShapeDtypeStruct((heads, 256), F32),
            jax.ShapeDtypeStruct((stretch, message), BF16),
        ],
        row_term,
        scalars=place,
        moved=2 << 20,
    )
    row_send = swapped(row_send, "col", 1)
    gradient = call(
        gradient_kernel, jax.ShapeDtypeStruct((own, rows, columns), F32), d_weights, moved=1 << 20
    )
    row_send, gradient = lax.optimization_barrier((row_send, gradient))
    inner = call(inner_kernel, jax.ShapeDtypeStruct((heads, 256), F32), [inner, row_send], moved=1 << 20)
    inners = [inner] + [swapped(inner, "seq", k) for k in range(1, seq_count)]
    score_cotangent = call(
        score_kernel,
        jax.ShapeDtypeStruct((own, rows, columns), F32),
        inners + [gradient, weights],
        scalars=place,
        moved=2 << 20,
    )
    alignment_cotangent = call(
        join_kernel,
        jax.ShapeDtypeStruct((sequences, stretch, features), F32),
        [row_keep, row_send, col_term],
        moved=2 << 20,
    )
    return (alignment_cotangent, score_cotangent)


def solution(mesh):
    return jax.shard_map(
        body,
        mesh=mesh,
        in_specs=(
            P("seq", "row", None),
            P("seq", "row", None),
            P("seq", "row"),
            P(),
            P(None, "row", "col"),
            P(),
            P(),
            P(),
        ),
        out_specs=(P("seq", ("row", "col"), None), P("seq", "row", "col")),
        check_vma=False,
    )
```

```python
import jax
import jax.numpy as jnp
from jax import lax
from jax.experimental import pallas as pl
from jax.experimental.pallas import tpu as pltpu
from jax.sharding import PartitionSpec as P

F32 = jnp.float32
BF16 = jnp.bfloat16
MASKED = -1000000000.0
VMEM_BYTES = 48 * 1024 * 1024
STEPS = 1


def call(kernel, outs, inputs, in_specs=None, out_specs=None, grid=None, scratch=(), scalars=None, flops=0, moved=0):
    local = lambda: pl.BlockSpec(memory_space=pltpu.VMEM)
    several = isinstance(outs, list)
    operands = [] if scalars is None else [scalars]
    if in_specs is None:
        in_specs = [local() for _ in inputs]
    if out_specs is None:
        out_specs = [local() for _ in outs] if several else local()
    extra = {} if grid is None else {"grid": grid}
    return pl.pallas_call(
        kernel,
        out_shape=outs,
        in_specs=[pl.BlockSpec(memory_space=pltpu.SMEM)] * len(operands) + in_specs,
        out_specs=out_specs,
        scratch_shapes=list(scratch),
        compiler_params=pltpu.CompilerParams(vmem_limit_bytes=VMEM_BYTES),
        cost_estimate=pl.CostEstimate(flops=flops, bytes_accessed=moved, transcendentals=0),
        **extra,
    )(*operands, *inputs)


def whole(shape):
    return pl.BlockSpec(shape, lambda i: (0,) * len(shape))


def by_step(*dims):
    return pl.BlockSpec(dims, lambda i: (i,) + (0,) * (len(dims) - 1))


def far(a):
    return pltpu.with_memory_space_constraint(a, pltpu.HBM)


def dot(a, b):
    return jnp.dot(a, b, preferred_element_type=F32)


def dot_last(a, b):
    return lax.dot_general(a, b, (((1,), (1,)), ((), ())), preferred_element_type=F32)


def turned(a):
    return a.astype(F32).T.astype(a.dtype)


def stats_kernel(scores_ref, keep_ref, stats_ref):
    heads, rows, _ = scores_ref.shape
    keep = keep_ref[...] > 0
    lane = lax.broadcasted_iota(jnp.int32, (rows, 128), 1)
    table = jnp.zeros((rows, 128), F32)
    for h in range(heads):
        masked = jnp.where(keep, scores_ref[h], MASKED)
        peak = jnp.max(masked, axis=1, keepdims=True)
        total = jnp.sum(jnp.exp(masked - peak), axis=1, keepdims=True)
        table = jnp.where(lane == h, peak, table)
        table = jnp.where(lane == heads + h, total, table)
    packed = table.T[0 : 2 * heads]
    for k in range(stats_ref.shape[0]):
        stats_ref[k] = packed


def project_rows(weight, pieces, out_ref, first):
    sequences = pieces.shape[0]
    chunks, stretch, _ = out_ref.shape
    features = weight.shape[0]
    for s in range(0, sequences, 2):
        pair = [dot(weight, pieces[s + k]) for k in (0, 1)]
        rows = jnp.concatenate(pair, axis=0).T.reshape(chunks, stretch, 2 * features)
        lanes = pl.ds(pl.multiple_of((first + s) * features, 128), 2 * features)
        out_ref[:, :, lanes] = rows.astype(out_ref.dtype)


def thirds(table):
    first = table.astype(BF16)
    rest = table - first.astype(F32)
    second = rest.astype(BF16)
    third = (rest - second.astype(F32)).astype(BF16)
    return jnp.concatenate([t.astype(F32) for t in (first, second, third)], axis=0).astype(BF16)


def joined(table):
    count = table.shape[0] // 3
    table = table.astype(F32)
    return table[0:count] + table[count : 2 * count] + table[2 * count : 3 * count]


def main_kernel(
    place_ref,
    scores_ref,
    keep_ref,
    stats_ref,
    x_ref,
    cot_ref,
    mask_ref,
    mine_ref,
    other_ref,
    payload_ref,
    gate_w_ref,
    final_w_ref,
    weights_ref,
    col_ref,
    row0_ref,
    row1_ref,
    row2_ref,
    row3_ref,
    pair0_ref,
    pair1_ref,
    pair2_ref,
    pair3_ref,
    wt,
    weights,
    wb,
    att,
    term,
    values,
    pieces,
    row_out,
    pair_sum,
    pair_out,
):
    step = pl.program_id(0)
    heads, rows, columns = scores_ref.shape
    group = x_ref.shape[0]
    width = payload_ref.shape[1]
    dim = width // heads
    wide = col_ref.shape[2]

    @pl.when(step == 0)
    def _():
        for k, weight in enumerate((payload_ref, gate_w_ref, final_w_ref)):
            wt[k] = turned(weight[...])
        pair_sum[...] = jnp.zeros(pair_sum.shape, F32)
        peaks = stats_ref[:, 0:heads]
        peak = jnp.max(peaks, axis=0)
        total = jnp.sum(stats_ref[:, heads : 2 * heads] * jnp.exp(peaks - peak[None]), axis=0)
        table = jnp.concatenate([peak, 1.0 / total, jnp.zeros((128 - 2 * heads, rows), F32)], axis=0).T
        keep = keep_ref[...] > 0
        for h in range(heads):
            masked = jnp.where(keep, scores_ref[h], MASKED)
            exact = jnp.exp(masked - table[:, h : h + 1]) * table[:, heads + h : heads + h + 1]
            weights[h] = exact
            wb[h] = exact.astype(BF16)

    first = pl.multiple_of(step * group, group)
    mask = mask_ref[...].astype(F32)
    for k in range(group):
        gate = 1.0 / (1.0 + jnp.exp(-dot(wt[1], x_ref[k])))
        cot = dot(wt[2], cot_ref[k]) * mask[k : k + 1]
        exact = cot * gate
        att[k] = exact.astype(BF16)
        term[k] = exact * (1.0 - gate)
    for h in range(heads):
        block = att[:, h * dim : (h + 1) * dim, :].reshape(group * dim, rows)
        pieces[:, h * dim : (h + 1) * dim, :] = dot(block, wb[h]).astype(BF16).reshape(group, dim, columns)
    project_rows(payload_ref[...], pieces, col_ref, first)

    own = place_ref[0] != place_ref[1]
    tokens = jnp.where(own, mine_ref[pl.ds(first, group)], other_ref[pl.ds(first, group)])
    for k in range(group):
        values[k] = dot(wt[0], tokens[k]).astype(BF16)
    for h in range(heads):
        block = values[:, h * dim : (h + 1) * dim, :].reshape(group * dim, columns)
        average = dot_last(block, wb[h]).reshape(group, dim, rows)
        pieces[:, h * dim : (h + 1) * dim, :] = (average * term[:, h * dim : (h + 1) * dim, :]).astype(BF16)
        att_rows = turned(att[:, h * dim : (h + 1) * dim, :].reshape(group * dim, rows))
        pair_sum[h] += dot(att_rows, block)
    project_rows(gate_w_ref[...], pieces, row_out, first)

    @pl.when(step == pl.num_programs(0) - 1)
    def _():
        lane = lax.broadcasted_iota(jnp.int32, (rows, 128), 1)
        table = jnp.zeros((rows, 128), F32)
        owners = pair_out.shape[0]
        own_heads = heads // owners
        for k in range(owners):
            tails = []
            for g in range(own_heads):
                h = k * own_heads + g
                grad = pair_sum[h].astype(BF16)
                pair_out[k, g] = grad[:, 0:128]
                tails.append(grad[:, 128:192])
                inner = jnp.sum(weights[h] * grad.astype(F32), axis=1, keepdims=True)
                table = jnp.where(lane == h, inner, table)
            pair_out[k, own_heads] = jnp.concatenate(tails, axis=-1)
        inner = thirds(jnp.concatenate([table.T[0:heads], jnp.zeros((heads, 256 - rows), F32)], axis=-1))
        for k, out_ref in enumerate((row0_ref, row1_ref, row2_ref, row3_ref)):
            out_ref[:, :, 0:wide] = row_out[pl.ds(2 * (place_ref[2] ^ k), 2)]
            for z in range(2):
                out_ref[z, :, wide:] = inner[:, 128 * z : 128 * z + 128]
        for k, out_ref in enumerate((pair0_ref, pair1_ref, pair2_ref, pair3_ref)):
            out_ref[...] = pair_out[place_ref[3] ^ k]
        weights_ref[...] = weights[pl.ds(place_ref[3] * own_heads, own_heads)]


def score_kernel(
    place_ref,
    part0_ref,
    part1_ref,
    part2_ref,
    part3_ref,
    inner0_ref,
    inner1_ref,
    inner2_ref,
    inner3_ref,
    weights_ref,
    out_ref,
):
    heads, rows, _ = out_ref.shape
    total = part0_ref[...].astype(F32)
    for part in (part1_ref, part2_ref, part3_ref):
        total = total + part[...].astype(F32)
    inner = ((inner0_ref[...] + inner1_ref[...]) + (inner2_ref[...] + inner3_ref[...]))[:, 0:rows]
    table = jnp.concatenate([inner, jnp.zeros((128 - inner.shape[0], rows), F32)], axis=0).T
    lane = lax.broadcasted_iota(jnp.int32, table.shape, 1)
    for h in range(heads):
        mine = place_ref[3] * heads + h
        grad = jnp.concatenate([total[h], total[heads][:, 64 * h : 64 * h + 64]], axis=-1)
        own = jnp.sum(jnp.where(lane == mine, table, 0.0), axis=1, keepdims=True)
        out_ref[h] = weights_ref[h] * (grad - own)


def total_kernel(parts_ref, out_ref):
    out_ref[...] = jnp.sum(parts_ref[...].astype(F32), axis=0).astype(BF16)


def fold_kernel(place_ref, part0_ref, part1_ref, part2_ref, part3_ref, keep_ref, inner_ref, send_ref):
    wide = keep_ref.shape[1]
    parts = (part0_ref, part1_ref, part2_ref, part3_ref)
    total = sum(part[:, :, 0:wide].astype(F32) for part in parts)
    high = place_ref[1] == 1
    keep_ref[...] = jnp.where(high, total[1], total[0])
    send_ref[:, 0:wide] = jnp.where(high, total[0], total[1]).astype(BF16)
    inner = sum(joined(jnp.concatenate([part[0, :, wide:], part[1, :, wide:]], axis=-1)) for part in parts)
    inner_ref[...] = inner
    send_ref[:, wide:] = thirds(inner)


def inner_kernel(inner_ref, rows_ref, out_ref):
    out_ref[...] = inner_ref[...] + joined(rows_ref[:, rows_ref.shape[1] - 256 :])


def join_kernel(keep_ref, rows_ref, cols_ref, out_ref):
    sequences, _, features = out_ref.shape
    total = keep_ref[...] + rows_ref[:, 0 : keep_ref.shape[1]].astype(F32) + cols_ref[...].astype(F32)
    for s in range(sequences):
        out_ref[s] = total[:, s * features : (s + 1) * features]


def body(
    layernormed_alignment,
    average_cotangent,
    sequence_validity,
    residue_validity,
    pair_scores,
    payload_projection,
    sigmoid_projection,
    final_projection,
):
    row_count = lax.axis_size("row")
    col_count = lax.axis_size("col")
    seq_count = lax.axis_size("seq")
    row_pos = lax.axis_index("row")
    col_pos = lax.axis_index("col")
    seq_pos = lax.axis_index("seq")
    sequences, rows, features = layernormed_alignment.shape
    heads, _, columns = pair_scores.shape
    width = payload_projection.shape[1]
    dim = width // heads
    stretch = rows // col_count
    wide = sequences * features
    own = heads // seq_count
    group = sequences // STEPS
    side = row_count // 2
    core, plane, across = row_pos % 2, col_pos % 2, col_pos // 2
    place = jnp.stack([core, plane, across, seq_pos]).astype(jnp.int32)

    tokens = far(jnp.swapaxes(layernormed_alignment, 1, 2))
    cotangent = far(jnp.swapaxes(average_cotangent, 1, 2))
    scores = far(pair_scores)
    payload_w = far(payload_projection)
    gate_w = far(sigmoid_projection)
    final_w = far(final_projection.T)
    keep = lax.dynamic_slice_in_dim(residue_validity, col_pos * columns, columns, 0).reshape(1, columns)

    at = lambda x, core, y, z: (x * 2 + core) * col_count + y * 2 + z
    routes = [
        (at(a, z, b, z), at((b + 2 * a) % side, 1 - z, a, z))
        for a in range(side)
        for b in range(side)
        for z in range(2)
    ]
    mine = lax.ppermute(jnp.swapaxes(layernormed_alignment, 1, 2), ("row", "col"), routes)

    local_stats = call(
        stats_kernel,
        jax.ShapeDtypeStruct((col_count, 2 * heads, rows), F32),
        [scores, keep],
        moved=4 << 20,
    )
    stats = lax.all_to_all(local_stats, "col", 0, 0, tiled=True)

    mine, stats = lax.optimization_barrier((mine, stats))
    other = lax.ppermute(mine, "row", [(i, i ^ 1) for i in range(row_count)])

    message = wide + 256
    half_message = wide + 128
    pieces = pltpu.VMEM((group, width, rows), BF16)
    square = pltpu.VMEM((heads, rows, columns), F32)
    weights, col_term, *sent = call(
        main_kernel,
        [jax.ShapeDtypeStruct((own, rows, columns), F32), jax.ShapeDtypeStruct((row_count, stretch, wide), BF16)]
        + [jax.ShapeDtypeStruct((2, stretch, half_message), BF16)]
        + [pltpu.HBM((2, stretch, half_message), BF16)] * (side - 1)
        + [jax.ShapeDtypeStruct((own + 1, rows, 128), BF16)] * seq_count,
        [scores, keep, stats, tokens, cotangent, far(sequence_validity), mine, other, payload_w, gate_w, final_w],
        [
            whole((heads, rows, columns)),
            whole((1, columns)),
            whole((col_count, 2 * heads, rows)),
            by_step(group, features, rows),
            by_step(group, features, rows),
            by_step(group, rows),
            whole((sequences, features, rows)),
            whole((sequences, features, rows)),
            whole((features, width)),
            whole((features, width)),
            whole((features, width)),
        ],
        [whole((own, rows, columns)), whole((row_count, stretch, wide))]
        + [whole((2, stretch, half_message)) for _ in range(side)]
        + [whole((own + 1, rows, 128)) for _ in range(seq_count)],
        grid=(STEPS,),
        scratch=[
            pltpu.VMEM((3, width, features), BF16),
            square,
            pltpu.VMEM((heads, rows, columns), BF16),
            pieces,
            pltpu.VMEM((group, width, rows), F32),
            pieces,
            pieces,
            pltpu.VMEM((col_count, stretch, wide), BF16),
            square,
            pltpu.VMEM((seq_count, own + 1, rows, 128), BF16),
        ],
        scalars=place,
        flops=1 << 30,
        moved=18 << 20,
    )
    row_term, d_weights = sent[:side], sent[side:]

    def swapped(a, axis, bits):
        return lax.ppermute(a, axis, [(i, i ^ bits) for i in range(lax.axis_size(axis))])

    row_term = row_term[:1] + [swapped(row_term[k], "col", 2 * k) for k in range(1, side)]
    d_weights = d_weights[:1] + [swapped(d_weights[k], "seq", k) for k in range(1, seq_count)]
    col_term = lax.all_to_all(col_term, "row", 0, 0, tiled=True)
    col_term = call(total_kernel, jax.ShapeDtypeStruct((stretch, wide), BF16), [col_term], moved=1 << 20)
    col_term, row_term[3] = lax.optimization_barrier((col_term, row_term[3]))
    col_term = lax.ppermute(
        col_term,
        ("row", "col"),
        [(r * col_count + c, c * col_count + r) for r in range(row_count) for c in range(col_count)],
    )
    row_keep, inner, row_send = call(
        fold_kernel,
        [
            jax.ShapeDtypeStruct((stretch, wide), F32),
            jax.ShapeDtypeStruct((heads, 256), F32),
            jax.ShapeDtypeStruct((stretch, message), BF16),
        ],
        row_term,
        scalars=place,
        moved=2 << 20,
    )
    row_send = swapped(row_send, "col", 1)
    inner = call(inner_kernel, jax.ShapeDtypeStruct((heads, 256), F32), [inner, row_send], moved=1 << 20)
    inners = [inner] + [swapped(inner, "seq", k) for k in range(1, seq_count)]
    score_cotangent = call(
        score_kernel,
        jax.ShapeDtypeStruct((own, rows, columns), F32),
        d_weights + inners + [weights],
        scalars=place,
        moved=2 << 20,
    )
    alignment_cotangent = call(
        join_kernel,
        jax.ShapeDtypeStruct((sequences, stretch, features), F32),
        [row_keep, row_send, col_term],
        moved=2 << 20,
    )
    return (alignment_cotangent, score_cotangent)


def solution(mesh):
    return jax.shard_map(
        body,
        mesh=mesh,
        in_specs=(
            P("seq", "row", None),
            P("seq", "row", None),
            P("seq", "row"),
            P(),
            P(None, "row", "col"),
            P(),
            P(),
            P(),
        ),
        out_specs=(P("seq", ("row", "col"), None), P("seq", "row", "col")),
        check_vma=False,
    )
```
